32 devices in a mesh: leaf: 4 (over y, x), row: 8 (over z, core).
Axes of the slice: x: 2, y: 2, z: 4, core: 2. Of those that a mesh axis runs over, the one named last changes fastest.
Arguments:
- right_side: bfloat16 [4, 32, 256, 512], P('leaf', 'row'), may hold values from -6 to 6
- panels: bfloat16 [4, 4, 32, 512, 512], P(None, 'leaf', 'row'), may hold values from -0.1875 to 0.1875
- tile_counts: int32 [4, 4, 32], P(None, 'leaf', 'row'), may hold values from 0 to 512, as said below
- diag_leaf: bfloat16 [4, 512, 512], P('leaf')
- diag_pair: bfloat16 [2, 512, 512], replicated
- diag_root: bfloat16 [2, 512, 512], replicated
- sup_rows: int32 [4], replicated, may hold values from 0 to 31, as said below
Outputs:
- solution: bfloat16 [4, 4, 256, 512], P(None, 'leaf')
- updated_side: bfloat16 [32, 256, 512], P('row')
The draws below stay inside these ranges and needn't reach their ends.
Inputs may be any that keep to these rules, and one draw needn't show every extreme that they name: `sup_rows`: 4 distinct block rows, one a level. `tile_counts`: 0 marks a tile with no valid columns.
All inputs are finite; a program needn't handle non-finite values.
Results may differ from the reference program's by a relative error of at most 0.0062.
Values may be sent and summed in bfloat16 or wider, within the bound.
No kernel may reach another device: no remote copies, remote signals or barrier semaphores. Data moves between devices by JAX's collectives and lax.ppermute only.
A program may use at most 128 MiB of HBM per device.

```python
import jax
import jax.numpy as jnp
from jax import lax

W = 512
R = 256
LEVELS = 4
TILES = 32
N_LEAF = 4


def near_identity(key, count):
    first_key = jax.random.fold_in(key, 0)
    noise = jax.random.normal(first_key, (count, W, W), jnp.float32) * (0.5 / W ** 0.5)
    return (jnp.eye(W, dtype=jnp.float32)[None] + noise).astype(jnp.bfloat16)


def draw_diag_leaf(key, part):
    return near_identity(jax.random.fold_in(key, 11), N_LEAF)


def draw_diag_pair(key, part):
    return near_identity(jax.random.fold_in(key, 12), N_LEAF // 2)


def draw_diag_root(key, part):
    return near_identity(jax.random.fold_in(key, 13), 2)


def draw_sup_rows(key, part):
    first_key, second_key = jax.random.split(jax.random.fold_in(key, 21))
    middle = jax.random.permutation(first_key, TILES - 2)[:LEVELS - 2] + 1
    picked_tiles = jnp.concatenate([jnp.array([0, TILES - 1], jnp.int32), middle.astype(jnp.int32)])
    shuffle = jax.random.permutation(second_key, LEVELS)
    return picked_tiles[shuffle].astype(jnp.int32)


def draw_tile_counts(key, part):
    first_key, second_key, third_key = jax.random.split(jax.random.fold_in(key, 31), 3)
    shape_all = (LEVELS, N_LEAF, TILES)
    counts_all = jax.random.randint(first_key, shape_all, 1, W + 1)
    empty_tile = jax.random.randint(second_key, shape_all, 0, 4) == 0
    counts_all = jnp.where(empty_tile, 0, counts_all).reshape(-1)
    chosen_slots = jax.random.permutation(third_key, LEVELS * N_LEAF * TILES)[:2]
    counts_all = counts_all.at[chosen_slots[0]].set(0).at[chosen_slots[1]].set(W)
    return counts_all.reshape(shape_all).astype(jnp.int32)


def level_of(own_key, shape, cuts, least, top_value):
    gain, own = 1.0, jax.random.fold_in(own_key, 6)
    for position, parts in cuts:
        steps = jnp.exp(jax.random.uniform(jax.random.fold_in(own, position), (parts,), jnp.float32, least / len(cuts), top_value / len(cuts)))
        gain = gain * jnp.repeat(steps, shape[position] // parts).reshape([-1 if axis == position else 1 for axis in range(len(shape))])
    return gain


def bell_draw(own_key, dims, width, most, cuts=(), held_as=jnp.bfloat16):
    result = width * jax.random.normal(own_key, dims, jnp.float32)
    if cuts:
        result = result * level_of(own_key, dims, cuts, -0.22, 0.18)
    return jnp.clip(result, -most, most).astype(held_as)


def setup_inputs(seed: int = 0) -> dict:
    key_of = jax.random.split(jax.random.key(seed), 8)
    right_side = bell_draw(key_of[0], (N_LEAF, TILES, R, W), 1.0, 6.0, ((0, 4), (1, 8)))
    panels = bell_draw(key_of[1], (LEVELS, N_LEAF, TILES, W, W), (2 * W) ** -0.5, 0.1875, ((1, 4), (2, 8)))
    tile_counts = draw_tile_counts(jax.random.fold_in(key_of[7], 71), 0)
    diag_leaf = draw_diag_leaf(jax.random.fold_in(key_of[7], 71), 0)
    diag_pair = draw_diag_pair(jax.random.fold_in(key_of[7], 71), 0)
    diag_root = draw_diag_root(jax.random.fold_in(key_of[7], 71), 0)
    sup_rows = draw_sup_rows(jax.random.fold_in(key_of[7], 71), 0)
    return dict(right_side=right_side, panels=panels, tile_counts=tile_counts, diag_leaf=diag_leaf, diag_pair=diag_pair, diag_root=diag_root, sup_rows=sup_rows)


def reference(right_side, panels, tile_counts, diag_leaf, diag_pair, diag_root, sup_rows):
    share_parts = right_side.astype(jnp.float32)
    totals = jnp.zeros(share_parts.shape, jnp.float32)
    tile_ids = jnp.arange(TILES, dtype=jnp.int32)
    columns = jnp.arange(W, dtype=jnp.int32)
    solved = []
    for panel_height in range(LEVELS):
        target_row = sup_rows[panel_height]
        partial_result = lax.dynamic_index_in_dim(share_parts, target_row, 1, keepdims=False) - lax.dynamic_index_in_dim(totals, target_row, 1, keepdims=False)
        if panel_height == 0:
            merged = partial_result
            inverse = diag_leaf
        elif panel_height == 1:
            merged = partial_result + partial_result[jnp.array([1, 0, 3, 2])]
            inverse = diag_pair[jnp.array([0, 0, 1, 1])]
        else:
            merged = jnp.broadcast_to(jnp.sum(partial_result, axis=0), partial_result.shape)
            inverse = jnp.broadcast_to(diag_root[panel_height - 2], (N_LEAF, W, W))
        rounded = lax.optimization_barrier(merged.astype(jnp.bfloat16)).astype(jnp.float32)
        current_solved = jnp.einsum("srw,swv->srv", rounded, inverse.astype(jnp.float32)).astype(jnp.bfloat16)
        solved.append(current_solved)
        structure = jnp.logical_not(jnp.any(tile_ids[:, None] == sup_rows[: panel_height + 1][None, :], axis=1))
        for current_leaf in range(N_LEAF):
            update_term = jnp.einsum("pi,bis->bps", current_solved[current_leaf].astype(jnp.float32), panels[panel_height, current_leaf].astype(jnp.float32))
            col_mask = (columns[None, :] < tile_counts[panel_height, current_leaf][:, None]) & structure[:, None]
            totals = totals.at[current_leaf].add(update_term * col_mask[:, None, :].astype(jnp.float32))
    solution = jnp.stack(solved)
    updated_side = jnp.sum(share_parts - totals, axis=0).astype(jnp.bfloat16)
    return solution, updated_side
```

```python
import jax
import jax.numpy as jnp
from jax import lax
from jax.sharding import PartitionSpec as P

F32 = jnp.float32
BF16 = jnp.bfloat16


def swap(block, axis, bits):
    return lax.ppermute(block, axis, [(i, i ^ bits) for i in range(lax.axis_size(axis))])


def dot(a, b):
    return jnp.dot(a, b, preferred_element_type=F32)


def piece(array, index, size, axis):
    return lax.dynamic_slice_in_dim(array, index * size, size, axis)


def placed(pieces, me, axis):
    size = pieces[0].shape[axis]
    shape = list(pieces[0].shape)
    shape[axis] = size * len(pieces)
    out = jnp.zeros(shape, pieces[0].dtype)
    for m, block in enumerate(pieces):
        out = lax.dynamic_update_slice_in_dim(out, block, (me ^ m) * size, axis)
    return out


def on_device(right_side, panels, tile_counts, diag_leaf, diag_pair, diag_root, sup_rows):
    right, panels, counts = right_side[0], panels[:, 0], tile_counts[:, 0]
    levels, here, width, _ = panels.shape
    n_row, n_leaf = lax.axis_size("row"), lax.axis_size("leaf")
    chips = min(n_row // 2, 4)
    leaf, row = lax.axis_index("leaf"), lax.axis_index("row")
    core, chip = row & 1, (row >> 1) & (chips - 1)
    outer = [1 << b for b in range(n_row.bit_length()) if 2 * chips <= 1 << b < n_row]
    half_r, half_w = right.shape[1] // 2, width // 2
    part_r, part_w = half_r // chips, width // chips

    ids = row * here + jnp.arange(here, dtype=jnp.int32)
    columns = jnp.arange(width, dtype=jnp.int32)
    masks = []
    for level in range(levels):
        free = jnp.all(ids[:, None] != sup_rows[None, : level + 1], axis=1)
        masks.append((columns[None, :] < counts[level][:, None]) & free[:, None])
    owned = [sup_rows[level] // here == row for level in range(levels)]
    local = [sup_rows[level] % here for level in range(levels)]

    def side(level):
        block = lax.dynamic_index_in_dim(right, local[level], 0, keepdims=False)
        return jnp.where(owned[level], block, jnp.zeros_like(block))

    def tile(of, level):
        block = lax.dynamic_index_in_dim(panels[of], local[level], 0, keepdims=False)
        mask = lax.dynamic_index_in_dim(masks[of], local[level], 0, keepdims=False)
        return jnp.where(mask[None, :] & owned[level], block, jnp.zeros_like(block))

    def spread(block):
        for bits in outer:
            block = block + swap(block, "row", bits)
        return block

    def halved(blocks, size):
        stack = jnp.stack(blocks)
        mine, other = piece(stack, core, size, 1), piece(stack, 1 - core, size, 1)
        return spread(mine + swap(other, "row", 1))

    def chip_scatter(block, size, axis):
        total = piece(block, chip, size, axis)
        for m in range(1, chips):
            total = total + swap(piece(block, chip ^ m, size, axis), "row", 2 * m)
        return total

    def chip_gather(block, axis):
        return placed([block] + [swap(block, "row", 2 * m) for m in range(1, chips)], chip, axis)

    def chip_spread(block):
        m = 1
        while m < chips:
            block = block + swap(block, "row", 2 * m)
            m *= 2
        return block

    def core_gather(block, axis):
        return placed([block, swap(block, "row", 1)], core, axis)

    sides = halved([side(level) for level in range(levels)], half_r)
    tiles = halved([tile(0, 1), tile(2, 3)], half_w)
    both = jnp.stack([tile(0, 2), tile(1, 2), tile(0, 3), tile(1, 3)])
    both = spread(both + swap(both, "row", 1))

    b0 = chip_spread(sides[0])
    level1 = chip_scatter(jnp.concatenate([tiles[0], sides[1]]), part_w, 1)
    p01 = core_gather(level1[:half_w], 0)
    b1 = level1[half_w:]

    x0 = dot(b0, diag_leaf[0]).astype(BF16)
    t1 = b1.astype(F32) - dot(x0, p01)
    m1 = (t1 + swap(t1, "leaf", 1)).astype(BF16)
    m1 = chip_gather(m1, 1)
    x1 = dot(m1, lax.dynamic_index_in_dim(diag_pair, leaf // 2, 0, keepdims=False)).astype(BF16)

    t2 = sides[2].astype(F32) - dot(x0, both[0]) - dot(x1, both[1])
    t3 = sides[3].astype(F32) - dot(x0, both[2]) - dot(x1, both[3])
    t23 = chip_scatter(jnp.concatenate([t2, t3], 1).astype(BF16), part_r, 0)
    total = t23.astype(F32)
    for m in range(1, n_leaf):
        total = total + swap(t23, "leaf", m).astype(F32)
    m23 = chip_gather(total.astype(BF16), 0)

    p23 = tiles[1].astype(F32)
    m = 1
    while m < n_leaf:
        p23 = p23 + swap(p23.astype(BF16), "leaf", m).astype(F32)
        m *= 2
    p23 = core_gather(chip_spread(p23.astype(BF16)), 0)

    x2 = dot(m23[:, :width], diag_root[0]).astype(BF16)
    x3 = dot((m23[:, width:].astype(F32) - dot(x2, p23)).astype(BF16), diag_root[1]).astype(BF16)

    x01 = core_gather(jnp.stack([x0, x1]), 1)
    x23 = core_gather(jnp.stack([x2, x3]), 1)

    def leaf_scatter(blocks, dims):
        first, second = dims
        keep = [piece(blocks, (leaf & (1 << first)) | (i << second), 1, 0) for i in range(2)]
        give = [piece(blocks, ((leaf ^ (1 << first)) & (1 << first)) | (i << second), 1, 0) for i in range(2)]
        got = swap(jnp.concatenate(give), "leaf", 1 << first)
        kept = (jnp.concatenate(keep).astype(F32) + got.astype(F32)).astype(BF16)
        bit = (leaf >> second) & 1
        mine, other = piece(kept, bit, 1, 0), piece(kept, 1 - bit, 1, 0)
        return (mine.astype(F32) + swap(other, "leaf", 1 << second).astype(F32)).astype(BF16)[0]

    sum2 = leaf_scatter(jnp.where(masks[2][:, None, :], panels[2], jnp.zeros_like(panels[2])), (0, 1))
    sum3 = leaf_scatter(jnp.where(masks[3][:, None, :], panels[3], jnp.zeros_like(panels[3])), (1, 0))

    update = right.astype(F32)
    for level in range(2):
        term = jnp.einsum("pi,bis->bps", x01[level], panels[level], preferred_element_type=F32)
        update = update - jnp.where(masks[level][:, None, :], term, jnp.zeros_like(term))
    update = update.astype(BF16)
    partial = piece(update, leaf, 1, 0)[0].astype(F32)
    for m in range(1, n_leaf):
        partial = partial + swap(piece(update, leaf ^ m, 1, 0)[0], "leaf", m).astype(F32)

    done = (partial - dot(x23[0], sum2) - dot(x23[1], sum3)).astype(BF16)[None]
    updated = placed([done] + [swap(done, "leaf", m) for m in range(1, n_leaf)], leaf, 0)
    return jnp.concatenate([x01, x23])[:, None], updated


def solution(mesh):
    return jax.shard_map(
        on_device,
        mesh=mesh,
        in_specs=(
            P("leaf", "row", None, None),
            P(None, "leaf", "row", None, None),
            P(None, "leaf", "row"),
            P("leaf", None, None),
            P(),
            P(),
            P(),
        ),
        out_specs=(P(None, "leaf", None, None), P("row", None, None)),
        check_vma=False,
    )
```

```python
import jax
import jax.numpy as jnp
from jax import lax
from jax.experimental import pallas as pl
from jax.experimental.pallas import tpu as pltpu
from jax.sharding import PartitionSpec as P

F32 = jnp.float32
BF16 = jnp.bfloat16
CORES = 2


def swap(block, axis, bits):
    return lax.ppermute(block, axis, [(i, i ^ bits) for i in range(lax.axis_size(axis))])


def dot(a, b):
    return jnp.dot(a, b, preferred_element_type=F32)


def shaped(shape, dtype=BF16):
    return jax.ShapeDtypeStruct(tuple(shape), dtype)


class Picked:
    def __init__(self, array, block, index):
        self.array, self.block, self.index = array, block, index


def on_device(right_side, panels, tile_counts, diag_leaf, diag_pair, diag_root, sup_rows):
    right, panels, counts = right_side[0], panels[:, 0], tile_counts[:, 0]
    levels, here, width, _ = panels.shape
    n_row, n_leaf = lax.axis_size("row"), lax.axis_size("leaf")
    chips = min(n_row // CORES, 4)
    outer = [1 << b for b in range(n_row.bit_length()) if CORES * chips <= 1 << b < n_row]
    height = right.shape[1]
    half_r, half_w = height // CORES, width // CORES
    part_r, part_w = half_r // chips, width // chips

    meta = jnp.concatenate(
        [
            jnp.stack([lax.axis_index("leaf"), lax.axis_index("row")]).astype(jnp.int32),
            sup_rows,
            counts.reshape(-1),
        ]
    )

    def leaf_of(meta):
        return meta[0]

    def core_of(meta):
        return meta[1] & (CORES - 1)

    def chip_of(meta):
        return (meta[1] // CORES) & (chips - 1)

    def spot(meta, level):
        return lax.rem(meta[2 + level], here)

    def owns(meta, level):
        return lax.div(meta[2 + level], here) == meta[1]

    def live(meta, level, a):
        kept = meta[2 + levels + level * here + a]
        for m in range(level + 1):
            kept = jnp.where(meta[1] * here + a == meta[2 + m], 0, kept)
        return kept

    def live_owned(meta, of, level):
        return jnp.where(owns(meta, level), live(meta, of, spot(meta, level)), 0)

    def keep(limit):
        ids = lax.broadcasted_iota(jnp.int32, (1, width), 1)
        return (ids < limit).astype(F32).astype(BF16)

    def side(level, other):
        return Picked(
            right,
            (None, half_r, width),
            lambda i, meta: (spot(meta, level), core_of(meta) ^ other, 0),
        )

    def side_value(meta, ref, level):
        return ref[...] * keep(jnp.where(owns(meta, level), width, 0))

    def tile(of, level, other=None):
        if other is None:
            return Picked(
                panels, (None, None, width, width), lambda i, meta: (of, spot(meta, level), 0, 0)
            )
        return Picked(
            panels,
            (None, None, half_w, width),
            lambda i, meta: (of, spot(meta, level), core_of(meta) ^ other, 0),
        )

    def tile_value(meta, ref, of, level):
        return ref[...] * keep(live_owned(meta, of, level))

    def run(body, operands, outs, scratch=(), steps=1, flops=0):
        arrays, specs, moved = [], [], 0
        for operand in operands:
            if not isinstance(operand, Picked):
                zeros = (0,) * operand.ndim
                operand = Picked(operand, operand.shape, lambda i, meta, zeros=zeros: zeros)
            arrays.append(operand.array)
            specs.append(pl.BlockSpec(operand.block, operand.index))
            size = operand.array.dtype.itemsize
            for n in operand.block:
                size *= n or 1
            moved += size * steps
        single = not isinstance(outs, (list, tuple))
        listed = [outs] if single else list(outs)
        out_specs = [
            pl.BlockSpec(out.shape, lambda i, meta, zeros=(0,) * len(out.shape): zeros)
            for out in listed
        ]
        moved += sum(out.size * out.dtype.itemsize for out in listed)
        results = pl.pallas_call(
            body,
            grid_spec=pltpu.PrefetchScalarGridSpec(
                num_scalar_prefetch=1,
                grid=(steps,),
                in_specs=specs,
                out_specs=out_specs,
                scratch_shapes=list(scratch),
            ),
            out_shape=listed,
            compiler_params=pltpu.CompilerParams(vmem_limit_bytes=40 * 1024 * 1024),
            cost_estimate=pl.CostEstimate(flops=flops, bytes_accessed=moved, transcendentals=0),
        )(meta, *arrays)
        return results[0] if single else results

    def spread(block):
        for bits in outer:
            block = block + swap(block, "row", bits)
        return block

    steps_up = [CORES * m for m in range(1, chips)]

    def b0_send(meta, ref, out):
        out[...] = side_value(meta, ref, 0)

    def b0_sum(meta, ref, got, out):
        out[...] = side_value(meta, ref, 0) + got[...]

    rows_half = shaped((half_r, width))
    b0 = run(b0_sum, [side(0, 0), swap(run(b0_send, [side(0, 1)], rows_half), "row", 1)], rows_half)
    b0 = spread(b0)
    bits = CORES
    while bits < CORES * chips // 2:
        b0 = b0 + swap(b0, "row", bits)
        bits *= 2
    b0_far = swap(b0, "row", bits)

    def first_send(meta, p, b, out):
        out[:half_w] = tile_value(meta, p, 0, 1)
        out[half_w:] = side_value(meta, b, 1)

    first = shaped((half_w + half_r, width))
    first_got = swap(run(first_send, [tile(0, 1, 1), side(1, 1)], first), "row", 1)

    def first_split(meta, p, b, got, *refs):
        outs, whole = refs[:-1], refs[-1]
        whole[:half_w] = tile_value(meta, p, 0, 1) + got[:half_w]
        whole[half_w:] = side_value(meta, b, 1) + got[half_w:]
        for m, out in enumerate(outs):
            start = pl.multiple_of((chip_of(meta) ^ m) * part_w, part_w)
            out[...] = whole[:, pl.ds(start, part_w)]

    columns = shaped((half_w + half_r, part_w))
    split = run(
        first_split,
        [tile(0, 1, 0), side(1, 0), first_got],
        [columns] * chips,
        [pltpu.VMEM((half_w + half_r, width), BF16)],
    )
    level1 = split[0]
    for piece, step in zip(split[1:], steps_up):
        level1 = level1 + swap(piece, "row", step)
    level1 = spread(level1)
    p01, b1 = level1[:half_w], level1[half_w:]
    p01_other = swap(p01, "row", 1)

    later = [(0, 2), (1, 2), (0, 3), (1, 3)]
    rest_rows = half_w + 2 * half_r + len(later) * width

    def rest_send(meta, p23, b2, b3, *refs):
        tiles, out = refs[:-1], refs[-1]
        out[:half_w] = tile_value(meta, p23, 2, 3)
        out[half_w : half_w + half_r] = side_value(meta, b2, 2)
        out[half_w + half_r : half_w + 2 * half_r] = side_value(meta, b3, 3)
        for i, (of, level) in enumerate(later):
            start = half_w + 2 * half_r + i * width
            out[start : start + width] = tile_value(meta, tiles[i], of, level)

    rest_got = swap(
        run(
            rest_send,
            [tile(2, 3, 1), side(2, 1), side(3, 1)] + [tile(*which) for which in later],
            shaped((rest_rows, width)),
        ),
        "row",
        1,
    )

    def x0_t1(meta, near, far, diag, p, p_other, b, x0, t1, whole):
        core = core_of(meta)
        x = dot(near[...] + far[...], diag[0]).astype(BF16)
        x0[...] = x
        whole[pl.ds(pl.multiple_of(core * half_w, half_w), half_w)] = p[...]
        whole[pl.ds(pl.multiple_of((1 - core) * half_w, half_w), half_w)] = p_other[...]
        t1[...] = b[...].astype(F32) - dot(x, whole[...])

    x0, t1 = run(
        x0_t1,
        [b0, b0_far, diag_leaf, p01, p01_other, b1],
        [rows_half, shaped((half_r, part_w), F32)],
        [pltpu.VMEM((width, part_w), BF16)],
    )
    m1 = (t1 + swap(t1, "leaf", 1)).astype(BF16)
    m1_parts = [m1] + [swap(m1, "row", step) for step in steps_up]

    def early(meta, p23, b2, b3, *refs):
        tiles, (got, x0), (p23_out, u, linked) = refs[:4], refs[4:6], refs[6:]
        p23_out[...] = tile_value(meta, p23, 2, 3) + got[:half_w]
        for i, b in enumerate((b2, b3)):
            rows = pl.ds(half_w + i * half_r, half_r)
            value = (side_value(meta, b, 2 + i) + got[rows]).astype(F32)
            start = half_w + 2 * half_r + 2 * i * width
            p0 = tile_value(meta, tiles[2 * i], 0, 2 + i) + got[start : start + width]
            u[:, i * width : (i + 1) * width] = value - dot(x0[...], p0)
            start += width
            linked[i] = tile_value(meta, tiles[2 * i + 1], 1, 2 + i) + got[start : start + width]

    p23, u, linked = run(
        early,
        [tile(2, 3, 0), side(2, 0), side(3, 0)]
        + [tile(*which) for which in later]
        + [rest_got, x0],
        [
            shaped((half_w, width)),
            shaped((half_r, 2 * width), F32),
            shaped((2, width, width)),
        ],
    )

    bits = 1
    while bits < n_leaf:
        p23 = (p23.astype(F32) + swap(p23, "leaf", bits).astype(F32)).astype(BF16)
        bits *= 2
    p23 = spread(p23)
    bits = CORES
    while bits < CORES * chips:
        p23 = p23 + swap(p23, "row", bits)
        bits *= 2
    p23_other = swap(p23, "row", 1)

    def x1_t23(meta, *refs):
        parts, (diag, u, linked, x1), rest = refs[:chips], refs[chips : chips + 4], refs[chips + 4 :]
        outs, whole = rest[:-1], rest[-1]
        chip = chip_of(meta)
        x = jnp.zeros((half_r, width), F32)
        for m, part in enumerate(parts):
            start = pl.multiple_of((chip ^ m) * part_w, part_w)
            x = x + dot(part[...], diag[pl.ds(start, part_w)])
        x = x.astype(BF16)
        x1[...] = x
        for i in range(2):
            cols = slice(i * width, (i + 1) * width)
            whole[:, cols] = u[:, cols] - dot(x, linked[i])
        for m, out in enumerate(outs):
            start = pl.multiple_of((chip ^ m) * part_r, part_r)
            out[...] = whole[pl.ds(start, part_r)].astype(BF16)

    pair = Picked(diag_pair, (None, width, width), lambda i, meta: (leaf_of(meta) // 2, 0, 0))
    strip = shaped((part_r, 2 * width))
    x1, *strips = run(
        x1_t23,
        m1_parts + [pair, u, linked],
        [rows_half] + [strip] * chips,
        [pltpu.VMEM((half_r, 2 * width), F32)],
    )
    t23 = strips[0]
    for piece, step in zip(strips[1:], steps_up):
        t23 = t23 + swap(piece, "row", step)
    t23 = spread(t23)
    total = t23.astype(F32)
    for m in range(1, n_leaf):
        total = total + swap(t23, "leaf", m).astype(F32)
    m23 = total.astype(BF16)
    m23_parts = [m23] + [swap(m23, "row", step) for step in steps_up]

    def x2_x3(meta, *refs):
        parts, (diag, p, p_other, out, whole, tile23) = refs[:chips], refs[chips:]
        chip, core = chip_of(meta), core_of(meta)
        for m, part in enumerate(parts):
            start = pl.multiple_of((chip ^ m) * part_r, part_r)
            whole[pl.ds(start, part_r)] = part[...]
        tile23[pl.ds(pl.multiple_of(core * half_w, half_w), half_w)] = p[...]
        tile23[pl.ds(pl.multiple_of((1 - core) * half_w, half_w), half_w)] = p_other[...]
        x = dot(whole[:, :width], diag[0]).astype(BF16)
        out[0] = x
        merged = whole[:, width:].astype(F32) - dot(x, tile23[...])
        out[1] = dot(merged.astype(BF16), diag[1]).astype(BF16)

    x23 = run(
        x2_x3,
        m23_parts + [diag_root, p23, p23_other],
        shaped((2, half_r, width)),
        [pltpu.VMEM((half_r, 2 * width), BF16), pltpu.VMEM((width, width), BF16)],
    )
    x01_other = [swap(x, "row", 1) for x in (x0, x1)]
    x23_other = swap(x23, "row", 1)

    def leaf_tile(array, level):
        if level is None:
            return Picked(
                array,
                (None, height, width),
                lambda i, meta: (leaf_of(meta) ^ lax.rem(i + 1, n_leaf), 0, 0),
            )
        return Picked(
            array,
            (None, None, width, width),
            lambda i, meta: (level, leaf_of(meta) ^ lax.rem(i + 1, n_leaf), 0, 0),
        )

    def update01(meta, b, pa, pb, x0, x1, x0_other, x1_other, *refs):
        outs, whole = refs[:-1], refs[-1]
        step = pl.program_id(0)
        core = core_of(meta)
        a = leaf_of(meta) ^ lax.rem(step + 1, n_leaf)

        @pl.when(step == 0)
        def _():
            for i, (mine, other) in enumerate(((x0, x0_other), (x1, x1_other))):
                whole[i, pl.ds(pl.multiple_of(core * half_r, half_r), half_r)] = mine[...]
                whole[i, pl.ds(pl.multiple_of((1 - core) * half_r, half_r), half_r)] = other[...]

        value = b[...].astype(F32)
        for i, p in enumerate((pa, pb)):
            value = value - dot(whole[i], p[...] * keep(live(meta, i, a)))
        for m in range(n_leaf):
            @pl.when(lax.rem(step + 1, n_leaf) == m)
            def _(m=m):
                outs[m][...] = value.astype(outs[m].dtype)

    block = shaped((height, width))
    shares = run(
        update01,
        [leaf_tile(right, None), leaf_tile(panels, 0), leaf_tile(panels, 1), x0, x1] + x01_other,
        [shaped((height, width), F32)] + [block] * (n_leaf - 1),
        [pltpu.VMEM((2, height, width), BF16)],
        steps=n_leaf,
    )
    shares_got = [swap(shares[m], "leaf", m) for m in range(1, n_leaf)]

    def panel_of(level, m):
        return Picked(
            panels,
            (None, None, width, width),
            lambda i, meta: (level, leaf_of(meta) ^ m, 0, 0),
        )

    def panel_value(meta, ref, level, m):
        return ref[...] * keep(live(meta, level, leaf_of(meta) ^ m))

    panels_got = []
    for m in range(1, n_leaf):
        def panel_send(meta, pa, pb, out, m=m):
            out[0] = panel_value(meta, pa, 2, m)
            out[1] = panel_value(meta, pb, 3, m)

        sent = run(panel_send, [panel_of(2, m), panel_of(3, m)], shaped((2, width, width)))
        panels_got.append(swap(sent, "leaf", m))

    def leaf_sums(meta, pa, pb, share, *refs):
        got, (panel_out, share_out) = refs[:-2], refs[-2:]
        panels_in, shares_in = got[: n_leaf - 1], got[n_leaf - 1 :]
        for i, p in enumerate((pa, pb)):
            value = panel_value(meta, p, 2 + i, 0).astype(F32)
            for ref in panels_in:
                value = value + ref[i].astype(F32)
            panel_out[i] = value.astype(BF16)
        value = share[...]
        for ref in shares_in:
            value = value + ref[...].astype(F32)
        share_out[...] = value

    panel_sum, share_sum = run(
        leaf_sums,
        [panel_of(2, 0), panel_of(3, 0), shares[0]] + panels_got + shares_got,
        [shaped((2, width, width)), shaped((height, width), F32)],
    )

    def final(meta, x0, x1, x0_other, x1_other, x23, x23_other, panel, share, solved, out):
        core = core_of(meta)
        mine = pl.ds(pl.multiple_of(core * half_r, half_r), half_r)
        other = pl.ds(pl.multiple_of((1 - core) * half_r, half_r), half_r)
        for i, (a, b) in enumerate(((x0, x0_other), (x1, x1_other))):
            solved[i, mine] = a[...]
            solved[i, other] = b[...]
        value = share[...]
        for i in range(2):
            solved[2 + i, mine] = x23[i]
            solved[2 + i, other] = x23_other[i]
            value = value - dot(solved[2 + i], panel[i])
        value = value.astype(BF16)
        for i in range(n_leaf):
            out[i] = value

    solved, done = run(
        final,
        [x0, x1] + x01_other + [x23, x23_other, panel_sum, share_sum],
        [shaped((levels, height, width)), shaped((n_leaf, height, width))],
    )
    updated = lax.all_to_all(done, "leaf", 0, 0, tiled=True)
    return solved[:, None], updated


def solution(mesh):
    return jax.shard_map(
        on_device,
        mesh=mesh,
        in_specs=(
            P("leaf", "row", None, None),
            P(None, "leaf", "row", None, None),
            P(None, "leaf", "row"),
            P("leaf", None, None),
            P(),
            P(),
            P(),
        ),
        out_specs=(P(None, "leaf", None, None), P("row", None, None)),
        check_vma=False,
    )
```

```python
import jax
import jax.numpy as jnp
from jax import lax
from jax.experimental import pallas as pl
from jax.experimental.pallas import tpu as pltpu
from jax.sharding import PartitionSpec as P

F32 = jnp.float32
BF16 = jnp.bfloat16
CORES = 2


def swap(block, axis, bits):
    return lax.ppermute(block, axis, [(i, i ^ bits) for i in range(lax.axis_size(axis))])


def dot(a, b):
    return jnp.dot(a, b, preferred_element_type=F32)


def shaped(shape, dtype=BF16):
    return jax.ShapeDtypeStruct(tuple(shape), dtype)


class Picked:
    def __init__(self, array, block, index):
        self.array, self.block, self.index = array, block, index


def on_device(right_side, panels, tile_counts, diag_leaf, diag_pair, diag_root, sup_rows):
    right, panels, counts = right_side[0], panels[:, 0], tile_counts[:, 0]
    levels, here, width, _ = panels.shape
    n_row, n_leaf = lax.axis_size("row"), lax.axis_size("leaf")
    chips = min(n_row // CORES, 4)
    outer = [1 << b for b in range(n_row.bit_length()) if CORES * chips <= 1 << b < n_row]
    height = right.shape[1]
    half_r, half_w = height // CORES, width // CORES
    part_r, part_w = half_r // chips, width // chips

    meta = jnp.concatenate(
        [
            jnp.stack([lax.axis_index("leaf"), lax.axis_index("row")]).astype(jnp.int32),
            sup_rows,
            counts.reshape(-1),
        ]
    )

    def leaf_of(meta):
        return meta[0]

    def core_of(meta):
        return meta[1] & (CORES - 1)

    def chip_of(meta):
        return (meta[1] // CORES) & (chips - 1)

    def spot(meta, level):
        return lax.rem(meta[2 + level], here)

    def owns(meta, level):
        return lax.div(meta[2 + level], here) == meta[1]

    def live(meta, level, a):
        kept = meta[2 + levels + level * here + a]
        for m in range(level + 1):
            kept = jnp.where(meta[1] * here + a == meta[2 + m], 0, kept)
        return kept

    def live_owned(meta, of, level):
        return jnp.where(owns(meta, level), live(meta, of, spot(meta, level)), 0)

    def keep(limit):
        ids = lax.broadcasted_iota(jnp.int32, (1, width), 1)
        return (ids < limit).astype(F32).astype(BF16)

    def side(level, other):
        return Picked(
            right,
            (None, half_r, width),
            lambda i, meta: (spot(meta, level), core_of(meta) ^ other, 0),
        )

    def side_value(meta, ref, level):
        return ref[...] * keep(jnp.where(owns(meta, level), width, 0))

    def tile(of, level, other=None):
        if other is None:
            return Picked(
                panels, (None, None, width, width), lambda i, meta: (of, spot(meta, level), 0, 0)
            )
        return Picked(
            panels,
            (None, None, half_w, width),
            lambda i, meta: (of, spot(meta, level), core_of(meta) ^ other, 0),
        )

    def tile_value(meta, ref, of, level):
        return ref[...] * keep(live_owned(meta, of, level))

    def run(body, operands, outs, scratch=(), steps=1, after=(), limit=40):
        arrays, specs, moved = [], [], 0
        for operand in operands:
            if not isinstance(operand, Picked):
                zeros = (0,) * operand.ndim
                operand = Picked(operand, operand.shape, lambda i, meta, zeros=zeros: zeros)
            arrays.append(operand.array)
            specs.append(pl.BlockSpec(operand.block, operand.index))
            size = operand.array.dtype.itemsize
            for n in operand.block:
                size *= n or 1
            moved += size * steps
        taken = len(arrays)
        arrays += after
        specs += [pl.BlockSpec(memory_space=pl.ANY)] * len(after)

        def kernel(meta, *refs):
            body(meta, *refs[:taken], *refs[taken + len(after) :])

        single = not isinstance(outs, (list, tuple))
        listed = [outs] if single else list(outs)
        out_specs = [
            pl.BlockSpec(out.shape, lambda i, meta, zeros=(0,) * len(out.shape): zeros)
            for out in listed
        ]
        moved += sum(out.size * out.dtype.itemsize for out in listed)
        results = pl.pallas_call(
            kernel,
            grid_spec=pltpu.PrefetchScalarGridSpec(
                num_scalar_prefetch=1,
                grid=(steps,),
                in_specs=specs,
                out_specs=out_specs,
                scratch_shapes=list(scratch),
            ),
            out_shape=listed,
            compiler_params=pltpu.CompilerParams(vmem_limit_bytes=limit * 1024 * 1024),
            cost_estimate=pl.CostEstimate(flops=0, bytes_accessed=moved, transcendentals=0),
        )(meta, *arrays)
        return results[0] if single else results

    def spread(block):
        for bits in outer:
            block = block + swap(block, "row", bits)
        return block

    steps_up = [CORES * m for m in range(1, chips)]
    rows_half = shaped((half_r, width))
    lanes = part_w
    blocks = width // lanes

    def at(index, size):
        return pl.ds(pl.multiple_of(index * size, size), size)

    first_rows = 2 * half_r + half_w

    def first_half(meta, out, b0, b1, p01, other):
        core = core_of(meta) ^ other
        out[:half_r] = b0[at(core, half_r)] * keep(jnp.where(owns(meta, 0), width, 0))
        out[half_r : 2 * half_r] = b1[at(core, half_r)] * keep(jnp.where(owns(meta, 1), width, 0))
        out[2 * half_r :] = p01[at(core, half_w)] * keep(live_owned(meta, 0, 1))

    def first_send(meta, b0, b1, p01, out):
        first_half(meta, out, b0, b1, p01, 1)

    def full_side(level):
        return Picked(right, (None, height, width), lambda i, meta: (spot(meta, level), 0, 0))

    first_in = [full_side(0), full_side(1), tile(0, 1)]
    first_got = swap(run(first_send, first_in, shaped((first_rows, width)), limit=60), "row", 1)

    b0_rows, column_rows = blocks * half_r, half_r + half_w
    near, far = (CORES, 2 * CORES)

    def first_split(meta, b0, b1, p01, got, send, kept, whole):
        first_half(meta, whole, b0, b1, p01, 0)
        whole[...] = whole[...] + got[...]
        for i in range(blocks):
            send[i * half_r : (i + 1) * half_r] = whole[:half_r, i * lanes : (i + 1) * lanes]
        kept[:b0_rows] = send[:b0_rows]
        chip = chip_of(meta)
        for i, (mine, other) in enumerate(((0, 1), (2, 3))):
            rows = slice(b0_rows + i * column_rows, b0_rows + (i + 1) * column_rows)
            send[rows] = whole[half_r:, at(chip ^ other, lanes)]
            kept[rows] = whole[half_r:, at(chip ^ mine, lanes)]

    near_shape = shaped((b0_rows + 2 * column_rows, lanes))
    near_send, near_kept = run(
        first_split,
        first_in + [first_got],
        [near_shape, near_shape],
        [pltpu.VMEM((first_rows, width), BF16)],
    )
    near_got = swap(spread(near_send), "row", near)
    near_kept = spread(near_kept)

    def first_join(meta, kept, got, send, own):
        send[:b0_rows] = kept[:b0_rows] + got[:b0_rows]
        middle = b0_rows + column_rows
        own[...] = kept[b0_rows:middle] + got[b0_rows:middle]
        send[b0_rows:] = kept[middle:] + got[middle:]

    far_send, columns_own = run(
        first_join,
        [near_kept, near_got],
        [shaped((b0_rows + column_rows, lanes)), shaped((column_rows, lanes))],
    )
    far_got = swap(far_send, "row", far)

    def panel_of(level, m):
        return Picked(
            panels,
            (None, None, width, width),
            lambda i, meta: (level, leaf_of(meta) ^ m, 0, 0),
        )

    def panel_value(meta, ref, level, m):
        return ref[...] * keep(live(meta, level, leaf_of(meta) ^ m))

    orders = ((2, 1, 2), (3, 2, 1))
    panel_got = []
    for level, one, two in orders:
        def panel_send(meta, pa, pb, out, level=level, one=one, two=two):
            out[0] = panel_value(meta, pa, level, one)
            out[1] = panel_value(meta, pb, level, one ^ two)

        sent = run(
            panel_send,
            [panel_of(level, one), panel_of(level, one ^ two)],
            shaped((2, width, width)),
            after=[near_send],
        )
        panel_got.append(swap(sent, "leaf", one))

    later = [(0, 2), (1, 2), (0, 3), (1, 3)]
    rest_rows = half_w + 2 * half_r + len(later) * width

    def rest_send(meta, p23, b2, b3, *refs):
        tiles, out = refs[:-1], refs[-1]
        out[:half_w] = tile_value(meta, p23, 2, 3)
        out[half_w : half_w + half_r] = side_value(meta, b2, 2)
        out[half_w + half_r : half_w + 2 * half_r] = side_value(meta, b3, 3)
        for i, (of, level) in enumerate(later):
            start = half_w + 2 * half_r + i * width
            out[start : start + width] = tile_value(meta, tiles[i], of, level)

    rest_got = swap(
        run(
            rest_send,
            [tile(2, 3, 1), side(2, 1), side(3, 1)] + [tile(*which) for which in later],
            shaped((rest_rows, width)),
            after=[near_send],
        ),
        "row",
        1,
    )

    def solve0(meta, sent, got, own, diag, x0, p, b):
        x = jnp.zeros((half_r, width), F32)
        for i in range(blocks):
            rows = slice(i * half_r, (i + 1) * half_r)
            x = x + dot(sent[rows] + got[rows], diag[0, i * lanes : (i + 1) * lanes])
        x0[...] = x.astype(BF16)
        b[...] = own[:half_r] + got[b0_rows : b0_rows + half_r]
        p[...] = own[half_r:] + got[b0_rows + half_r :]

    x0, p01, b1 = run(
        solve0,
        [far_send, far_got, columns_own, diag_leaf],
        [rows_half, shaped((half_w, lanes)), shaped((half_r, lanes))],
    )
    p01_other = swap(p01, "row", 1)

    def term1(meta, x0, p, p_other, b, t1, whole):
        core = core_of(meta)
        whole[at(core, half_w)] = p[...]
        whole[at(1 - core, half_w)] = p_other[...]
        t1[...] = b[...].astype(F32) - dot(x0[...], whole[...])

    t1 = run(
        term1,
        [x0, p01, p01_other, b1],
        shaped((half_r, lanes), F32),
        [pltpu.VMEM((width, lanes), BF16)],
    )
    m1 = (t1 + swap(t1, "leaf", 1)).astype(BF16)
    m1_parts = [m1] + [swap(m1, "row", step) for step in steps_up]

    def early(meta, p23, b2, b3, *refs):
        tiles, (got, x0), (p23_send, p23_kept, u, linked, whole) = refs[:4], refs[4:6], refs[6:]
        whole[...] = tile_value(meta, p23, 2, 3) + got[:half_w]
        chip = chip_of(meta)
        for i, (mine, other) in enumerate(((0, 1), (2, 3))):
            rows = slice(i * half_w, (i + 1) * half_w)
            p23_send[rows] = whole[:, at(chip ^ other, lanes)]
            p23_kept[rows] = whole[:, at(chip ^ mine, lanes)]
        for i, b in enumerate((b2, b3)):
            rows = slice(half_w + i * half_r, half_w + (i + 1) * half_r)
            value = (side_value(meta, b, 2 + i) + got[rows]).astype(F32)
            start = half_w + 2 * half_r + 2 * i * width
            p0 = tile_value(meta, tiles[2 * i], 0, 2 + i) + got[start : start + width]
            u[:, i * width : (i + 1) * width] = value - dot(x0[...], p0)
            start += width
            linked[i] = tile_value(meta, tiles[2 * i + 1], 1, 2 + i) + got[start : start + width]

    p23_pair = shaped((2 * half_w, lanes))
    p23_send, p23_kept, u, linked = run(
        early,
        [tile(2, 3, 0), side(2, 0), side(3, 0)]
        + [tile(*which) for which in later]
        + [rest_got, x0],
        [p23_pair, p23_pair, shaped((half_r, 2 * width), F32), shaped((2, width, width))],
        [pltpu.VMEM((half_w, width), BF16)],
        after=[t1],
    )

    p23_near = swap(spread(p23_send), "row", near)

    def p23_join(meta, kept, got, send, own):
        own[...] = kept[:half_w] + got[:half_w]
        send[...] = kept[half_w:] + got[half_w:]

    p23_block = shaped((half_w, lanes))
    p23_send, p23_own = run(p23_join, [spread(p23_kept), p23_near], [p23_block, p23_block])
    p23 = p23_own + swap(p23_send, "row", far)
    bits = 1
    while bits < n_leaf:
        p23 = (p23.astype(F32) + swap(p23, "leaf", bits).astype(F32)).astype(BF16)
        bits *= 2
    p23_parts = [p23] + [swap(p23, "row", step) for step in steps_up]

    def p23_place(meta, *refs):
        parts, out = refs[:-1], refs[-1]
        for m, part in enumerate(parts):
            out[:, at(chip_of(meta) ^ m, lanes)] = part[...]

    p23_half = run(p23_place, p23_parts, shaped((half_w, width)))
    p23_other = swap(p23_half, "row", 1)

    def x1_t23(meta, *refs):
        parts, (diag, u, linked, x1), rest = refs[:chips], refs[chips : chips + 4], refs[chips + 4 :]
        outs, whole = rest[:-1], rest[-1]
        chip = chip_of(meta)
        x = jnp.zeros((half_r, width), F32)
        for m, part in enumerate(parts):
            x = x + dot(part[...], diag[at(chip ^ m, lanes)])
        x = x.astype(BF16)
        x1[...] = x
        for i in range(2):
            cols = slice(i * width, (i + 1) * width)
            whole[:, cols] = u[:, cols] - dot(x, linked[i])
        for m, out in enumerate(outs):
            out[...] = whole[at(chip ^ m, part_r)].astype(BF16)

    pair = Picked(diag_pair, (None, width, width), lambda i, meta: (leaf_of(meta) // 2, 0, 0))
    strip = shaped((part_r, 2 * width))
    x1, *strips = run(
        x1_t23,
        m1_parts + [pair, u, linked],
        [rows_half] + [strip] * chips,
        [pltpu.VMEM((half_r, 2 * width), F32)],
    )
    t23 = strips[0]
    for piece, step in zip(strips[1:], steps_up):
        t23 = t23 + swap(piece, "row", step)
    t23 = spread(t23)
    total = t23.astype(F32)
    for m in range(1, n_leaf):
        total = total + swap(t23, "leaf", m).astype(F32)
    m23 = total.astype(BF16)
    m23_parts = [m23] + [swap(m23, "row", step) for step in steps_up]

    panel_far = []
    for (level, one, two), got in zip(orders, panel_got):
        def panel_join(meta, p, got, out, level=level, two=two):
            value = panel_value(meta, p, level, two).astype(F32) + got[1].astype(F32)
            out[...] = value.astype(BF16)

        sent = run(
            panel_join, [panel_of(level, two), got], shaped((width, width)), after=[p23_own, m1]
        )
        panel_far.append(swap(sent, "leaf", two))

    def x2_x3(meta, *refs):
        parts, (diag, p, p_other, out, whole, tile23) = refs[:chips], refs[chips:]
        chip, core = chip_of(meta), core_of(meta)
        for m, part in enumerate(parts):
            whole[at(chip ^ m, part_r)] = part[...]
        tile23[at(core, half_w)] = p[...]
        tile23[at(1 - core, half_w)] = p_other[...]
        x = dot(whole[:, :width], diag[0]).astype(BF16)
        out[0] = x
        merged = whole[:, width:].astype(F32) - dot(x, tile23[...])
        out[1] = dot(merged.astype(BF16), diag[1]).astype(BF16)

    x23 = run(
        x2_x3,
        m23_parts + [diag_root, p23_half, p23_other],
        shaped((2, half_r, width)),
        [pltpu.VMEM((half_r, 2 * width), BF16), pltpu.VMEM((width, width), BF16)],
    )
    x01_other = [swap(x, "row", 1) for x in (x0, x1)]
    x23_other = swap(x23, "row", 1)

    ways = ((1, 2), (2, 1))

    def leaf_tile(array, level):
        if level is None:
            return Picked(array, (None, height, width), lambda i, meta: (leaf_of(meta) ^ i, 0, 0))
        return Picked(
            array, (None, None, width, width), lambda i, meta: (level, leaf_of(meta) ^ i, 0, 0)
        )

    def update01(meta, b, pa, pb, x0, x1, x0_other, x1_other, *refs):
        sends, kept, whole = refs[:2], refs[2:4], refs[4]
        step = pl.program_id(0)
        core = core_of(meta)
        a = leaf_of(meta) ^ step

        @pl.when(step == 0)
        def _():
            for i, (mine, other) in enumerate(((x0, x0_other), (x1, x1_other))):
                whole[i, at(core, half_r)] = mine[...]
                whole[i, at(1 - core, half_r)] = other[...]

        value = b[...].astype(F32)
        for i, p in enumerate((pa, pb)):
            value = value - dot(whole[i], p[...] * keep(live(meta, i, a)))
        for half, (one, two) in enumerate(ways):
            part = value[half * half_r : (half + 1) * half_r]
            for i, m in enumerate((one, one ^ two)):
                @pl.when(step == m)
                def _(half=half, i=i, part=part):
                    sends[half][i] = part.astype(BF16)
            for i, m in enumerate((0, two)):
                @pl.when(step == m)
                def _(half=half, i=i, part=part):
                    kept[half][i] = part

    share_pair = (2, half_r, width)
    share_send0, share_send1, share_kept0, share_kept1 = run(
        update01,
        [leaf_tile(right, None), leaf_tile(panels, 0), leaf_tile(panels, 1), x0, x1] + x01_other,
        [shaped(share_pair)] * 2 + [shaped(share_pair, F32)] * 2,
        [pltpu.VMEM((2, height, width), BF16)],
        steps=n_leaf,
        after=[t23],
    )
    share_got = [swap(share_send0, "leaf", ways[0][0]), swap(share_send1, "leaf", ways[1][0])]

    def share_join(meta, kept0, kept1, got0, got1, out0, out1):
        for kept, got, out in ((kept0, got0, out0), (kept1, got1, out1)):
            out[...] = (kept[1] + got[1].astype(F32)).astype(BF16)

    share_sent = run(
        share_join, [share_kept0, share_kept1] + share_got, [shaped((half_r, width))] * 2
    )
    share_far = [swap(sent, "leaf", way[1]) for sent, way in zip(share_sent, ways)]

    def leaf_sums(meta, pa, pb, ga, gb, fa, fb, k0, k1, g0, g1, f0, f1, panel_out, share_out):
        for i, (p, got, far) in enumerate(((pa, ga, fa), (pb, gb, fb))):
            value = panel_value(meta, p, 2 + i, 0).astype(F32)
            panel_out[i] = (value + got[0].astype(F32) + far[...].astype(F32)).astype(BF16)
        for i, (kept, got, far) in enumerate(((k0, g0, f0), (k1, g1, f1))):
            value = kept[0] + got[0].astype(F32) + far[...].astype(F32)
            share_out[i * half_r : (i + 1) * half_r] = value

    panel_sum, share_sum = run(
        leaf_sums,
        [panel_of(2, 0), panel_of(3, 0)]
        + panel_got
        + panel_far
        + [share_kept0, share_kept1]
        + share_got
        + share_far,
        [shaped((2, width, width)), shaped((height, width), F32)],
    )

    def final(meta, x0, x1, x0_other, x1_other, x23, x23_other, panel, share, solved, out):
        core = core_of(meta)
        mine, other = at(core, half_r), at(1 - core, half_r)
        for i, (a, b) in enumerate(((x0, x0_other), (x1, x1_other))):
            solved[i, mine] = a[...]
            solved[i, other] = b[...]
        value = share[...]
        for i in range(2):
            solved[2 + i, mine] = x23[i]
            solved[2 + i, other] = x23_other[i]
            value = value - dot(solved[2 + i], panel[i])
        value = value.astype(BF16)
        for i in range(n_leaf):
            out[i] = value

    solved, done = run(
        final,
        [x0, x1] + x01_other + [x23, x23_other, panel_sum, share_sum],
        [shaped((levels, height, width)), shaped((n_leaf, height, width))],
    )
    updated = lax.all_to_all(done, "leaf", 0, 0, tiled=True)
    return solved[:, None], updated


def solution(mesh):
    return jax.shard_map(
        on_device,
        mesh=mesh,
        in_specs=(
            P("leaf", "row", None, None),
            P(None, "leaf", "row", None, None),
            P(None, "leaf", "row"),
            P("leaf", None, None),
            P(),
            P(),
            P(),
        ),
        out_specs=(P(None, "leaf", None, None), P("row", None, None)),
        check_vma=False,
    )
```

```python
import jax
import jax.numpy as jnp
from jax import lax
from jax.experimental import pallas as pl
from jax.experimental.pallas import tpu as pltpu
from jax.sharding import PartitionSpec as P

F32 = jnp.float32
BF16 = jnp.bfloat16
CORES = 2


def swap(block, axis, bits):
    return lax.ppermute(block, axis, [(i, i ^ bits) for i in range(lax.axis_size(axis))])


def dot(a, b):
    return jnp.dot(a, b, preferred_element_type=F32)


def shaped(shape, dtype=BF16):
    return jax.ShapeDtypeStruct(tuple(shape), dtype)


class Picked:
    def __init__(self, array, block, index):
        self.array, self.block, self.index = array, block, index


def on_device(right_side, panels, tile_counts, diag_leaf, diag_pair, diag_root, sup_rows):
    right, panels, counts = right_side[0], panels[:, 0], tile_counts[:, 0]
    levels, here, width, _ = panels.shape
    n_row, n_leaf = lax.axis_size("row"), lax.axis_size("leaf")
    chips = min(n_row // CORES, 4)
    outer = [1 << b for b in range(n_row.bit_length()) if CORES * chips <= 1 << b < n_row]
    height = right.shape[1]
    half_r, half_w = height // CORES, width // CORES
    part_r, part_w = half_r // chips, width // chips

    def row_of(meta):
        return lax.axis_index("row")

    def leaf_of(meta):
        return lax.axis_index("leaf")

    def core_of(meta):
        return row_of(meta) & (CORES - 1)

    def chip_of(meta):
        return lax.div(row_of(meta), CORES) & (chips - 1)

    def spot(meta, level):
        return lax.rem(meta[0][level], here)

    def owns(meta, level):
        return lax.div(meta[0][level], here) == row_of(meta)

    def live(meta, level, a):
        kept = meta[1][level, a]
        for m in range(level + 1):
            kept = jnp.where(row_of(meta) * here + a == meta[0][m], 0, kept)
        return kept

    def live_owned(meta, of, level):
        return jnp.where(owns(meta, level), live(meta, of, spot(meta, level)), 0)

    def keep(limit):
        ids = lax.broadcasted_iota(jnp.int32, (1, width), 1)
        return (ids < limit).astype(F32).astype(BF16)

    def side(level, other):
        return Picked(
            right,
            (None, half_r, width),
            lambda i, *meta: (spot(meta, level), core_of(meta) ^ other, 0),
        )

    def side_value(meta, ref, level):
        return ref[...] * keep(jnp.where(owns(meta, level), width, 0))

    def tile(of, level, other=None):
        if other is None:
            return Picked(
                panels, (None, None, width, width), lambda i, *meta: (of, spot(meta, level), 0, 0)
            )
        return Picked(
            panels,
            (None, None, half_w, width),
            lambda i, *meta: (of, spot(meta, level), core_of(meta) ^ other, 0),
        )

    def tile_value(meta, ref, of, level):
        return ref[...] * keep(live_owned(meta, of, level))

    def run(body, operands, outs, scratch=(), steps=1, after=(), limit=32):
        arrays, specs, moved = [], [], 0
        for operand in operands:
            if not isinstance(operand, Picked):
                zeros = (0,) * operand.ndim
                operand = Picked(operand, operand.shape, lambda i, sup, live_counts, zeros=zeros: zeros)
            arrays.append(operand.array)
            specs.append(pl.BlockSpec(operand.block, operand.index))
            size = operand.array.dtype.itemsize
            for n in operand.block:
                size *= n or 1
            moved += size * steps
        taken = len(arrays)
        arrays += list(after)
        specs += [pl.BlockSpec(memory_space=pl.ANY)] * len(after)

        def kernel(sup, live_counts, *refs):
            body((sup, live_counts), *refs[:taken], *refs[taken + len(after) :])

        single = not isinstance(outs, (list, tuple))
        listed = [outs] if single else list(outs)
        out_specs = [
            pl.BlockSpec(out.shape, lambda i, sup, live_counts, zeros=(0,) * len(out.shape): zeros)
            for out in listed
        ]
        moved += sum(out.size * out.dtype.itemsize for out in listed)
        results = pl.pallas_call(
            kernel,
            grid_spec=pltpu.PrefetchScalarGridSpec(
                num_scalar_prefetch=2,
                grid=(steps,),
                in_specs=specs,
                out_specs=out_specs,
                scratch_shapes=list(scratch),
            ),
            out_shape=listed,
            name=body.__name__,
            compiler_params=pltpu.CompilerParams(vmem_limit_bytes=limit * 1024 * 1024),
            cost_estimate=pl.CostEstimate(flops=0, bytes_accessed=moved, transcendentals=0),
        )(sup_rows, counts, *arrays)
        return results[0] if single else results

    def spread(block):
        for bits in outer:
            block = block + swap(block, "row", bits)
        return block

    steps_up = [CORES * m for m in range(1, chips)]
    rows_half = shaped((half_r, width))
    lanes = part_w
    blocks = width // lanes

    def at(index, size):
        return pl.ds(pl.multiple_of(index * size, size), size)

    first_rows = 2 * half_r + 2 * half_w

    def first_half(meta, out, b0, b1, p01, p23):
        out[:half_r] = side_value(meta, b0, 0)
        out[half_r : 2 * half_r] = side_value(meta, b1, 1)
        out[2 * half_r : 2 * half_r + half_w] = tile_value(meta, p01, 0, 1)
        out[2 * half_r + half_w :] = tile_value(meta, p23, 2, 3)

    def first_send(meta, b0, b1, p01, p23, out):
        first_half(meta, out, b0, b1, p01, p23)

    def first_in(other):
        return [side(0, other), side(1, other), tile(0, 1, other), tile(2, 3, other)]

    first_got = swap(run(first_send, first_in(1), shaped((first_rows, width)), limit=60), "row", 1)

    b0_rows, column_rows = blocks * half_r, half_r + half_w
    near, far = (CORES, 2 * CORES)

    def first_split(meta, b0, b1, p01, p23, got, send, kept, p23_send, p23_kept, whole):
        first_half(meta, whole, b0, b1, p01, p23)
        whole[...] = whole[...] + got[...]
        for i in range(blocks):
            send[i * half_r : (i + 1) * half_r] = whole[:half_r, i * lanes : (i + 1) * lanes]
        kept[:b0_rows] = send[:b0_rows]
        chip = chip_of(meta)
        for i, (mine, other) in enumerate(((0, 1), (2, 3))):
            rows = slice(b0_rows + i * column_rows, b0_rows + (i + 1) * column_rows)
            source = slice(half_r, half_r + column_rows)
            send[rows] = whole[source, at(chip ^ other, lanes)]
            kept[rows] = whole[source, at(chip ^ mine, lanes)]
            rows = slice(i * half_w, (i + 1) * half_w)
            source = slice(half_r + column_rows, first_rows)
            p23_send[rows] = whole[source, at(chip ^ other, lanes)]
            p23_kept[rows] = whole[source, at(chip ^ mine, lanes)]

    near_shape, p23_pair = (
        shaped((b0_rows + 2 * column_rows, lanes)),
        shaped((2 * half_w, lanes)),
    )
    near_send, near_kept, p23_send, p23_kept = run(
        first_split,
        first_in(0) + [first_got],
        [near_shape, near_shape, p23_pair, p23_pair],
        [pltpu.VMEM((first_rows, width), BF16)],
    )
    near_got = swap(spread(near_send), "row", near)
    near_kept = spread(near_kept)
    p23_got = swap(spread(p23_send), "row", near)
    p23_kept = spread(p23_kept)

    def first_join(meta, kept, got, send, own):
        send[:b0_rows] = kept[:b0_rows] + got[:b0_rows]
        middle = b0_rows + column_rows
        own[...] = kept[b0_rows:middle] + got[b0_rows:middle]
        send[b0_rows:] = kept[middle:] + got[middle:]

    far_send, columns_own = run(
        first_join,
        [near_kept, near_got],
        [shaped((b0_rows + column_rows, lanes)), shaped((column_rows, lanes))],
    )
    far_got = swap(far_send, "row", far)

    def p23_join(meta, kept, got, send, own):
        own[...] = kept[:half_w] + got[:half_w]
        send[...] = kept[half_w:] + got[half_w:]

    p23_block = shaped((half_w, lanes))
    p23_send, p23_own = run(
        p23_join, [p23_kept, p23_got], [p23_block, p23_block], after=[far_send]
    )
    p23_far = swap(p23_send, "row", far)

    def panel_of(level, m):
        return Picked(
            panels,
            (None, None, width, width),
            lambda i, *meta: (level, leaf_of(meta) ^ m, 0, 0),
        )

    def panel_value(meta, ref, level, m):
        return ref[...] * keep(live(meta, level, leaf_of(meta) ^ m))

    orders = ((2, 1, 2), (3, 2, 1))
    panel_got = []
    for level, one, two in orders:
        def panel_send(meta, pa, pb, out, level=level, one=one, two=two):
            out[0] = panel_value(meta, pa, level, one)
            out[1] = panel_value(meta, pb, level, one ^ two)

        sent = run(
            panel_send,
            [panel_of(level, one), panel_of(level, one ^ two)],
            shaped((2, width, width)),
            after=[near_send],
        )
        panel_got.append(swap(sent, "leaf", one))

    later = [(0, 2), (1, 2), (0, 3), (1, 3)]
    rest_rows = 2 * half_r + len(later) * width

    def rest_send(meta, b2, b3, *refs):
        tiles, out = refs[:-1], refs[-1]
        out[:half_r] = side_value(meta, b2, 2)
        out[half_r : 2 * half_r] = side_value(meta, b3, 3)
        for i, (of, level) in enumerate(later):
            start = 2 * half_r + i * width
            out[start : start + width] = tile_value(meta, tiles[i], of, level)

    rest_got = swap(
        run(
            rest_send,
            [side(2, 1), side(3, 1)] + [tile(*which) for which in later],
            shaped((rest_rows, width)),
            after=[near_send],
        ),
        "row",
        1,
    )

    def solve0(meta, sent, got, own, diag, x0, p, b):
        x = jnp.zeros((half_r, width), F32)
        for i in range(blocks):
            rows = slice(i * half_r, (i + 1) * half_r)
            x = x + dot(sent[rows] + got[rows], diag[0, i * lanes : (i + 1) * lanes])
        x0[...] = x.astype(BF16)
        b[...] = own[:half_r] + got[b0_rows : b0_rows + half_r]
        p[...] = own[half_r:] + got[b0_rows + half_r :]

    x0, p01, b1 = run(
        solve0,
        [far_send, far_got, columns_own, diag_leaf],
        [rows_half, shaped((half_w, lanes)), shaped((half_r, lanes))],
        after=[p23_send],
    )
    p01_other = swap(p01, "row", 1)

    def term1(meta, x0, p, p_other, b, t1, whole):
        core = core_of(meta)
        whole[at(core, half_w)] = p[...]
        whole[at(1 - core, half_w)] = p_other[...]
        t1[...] = b[...].astype(F32) - dot(x0[...], whole[...])

    t1 = run(
        term1,
        [x0, p01, p01_other, b1],
        shaped((half_r, lanes), F32),
        [pltpu.VMEM((width, lanes), BF16)],
        after=[p23_far],
    )
    panel_far, panel_sent = [], []
    for (level, one, two), got in zip(orders, panel_got):
        def panel_join(meta, p, got, out, level=level, two=two):
            value = panel_value(meta, p, level, two).astype(F32) + got[1].astype(F32)
            out[...] = value.astype(BF16)

        sent = run(
            panel_join, [panel_of(level, two), got], shaped((width, width)), after=[t1]
        )
        panel_sent.append(sent)
        panel_far.append(swap(sent, "leaf", two))

    p23 = p23_own + p23_far
    p23 = (p23.astype(F32) + swap(p23, "leaf", 1).astype(F32)).astype(BF16)
    p23_turned = swap(p23, "leaf", 2)

    def m1_sum(meta, a, b, out):
        out[...] = (a[...] + b[...]).astype(BF16)

    m1 = run(m1_sum, [t1, swap(t1, "leaf", 1)], shaped((half_r, lanes)), after=panel_sent)
    m1 = jnp.concatenate([m1, swap(m1, "row", near)])
    m1_far = swap(m1, "row", far)
    p23 = (p23.astype(F32) + p23_turned.astype(F32)).astype(BF16)
    p23 = jnp.concatenate([p23, swap(p23, "row", near)])
    p23_far = swap(p23, "row", far)

    def p23_place(meta, near_two, far_two, out):
        for m in range(chips):
            source = (near_two, far_two)[m // 2]
            rows = slice((m % 2) * half_w, (m % 2 + 1) * half_w)
            out[:, at(chip_of(meta) ^ m, lanes)] = source[rows]

    p23_half = run(p23_place, [p23, p23_far], shaped((half_w, width)))
    p23_other = swap(p23_half, "row", 1)

    def early(meta, b2, b3, *refs):
        tiles, (got, x0, u, linked) = refs[:4], refs[4:]
        for i, b in enumerate((b2, b3)):
            rows = slice(i * half_r, (i + 1) * half_r)
            value = (side_value(meta, b, 2 + i) + got[rows]).astype(F32)
            start = 2 * half_r + 2 * i * width
            p0 = tile_value(meta, tiles[2 * i], 0, 2 + i) + got[start : start + width]
            u[:, i * width : (i + 1) * width] = value - dot(x0[...], p0)
            start += width
            linked[i] = tile_value(meta, tiles[2 * i + 1], 1, 2 + i) + got[start : start + width]

    u, linked = run(
        early,
        [side(2, 0), side(3, 0)] + [tile(*which) for which in later] + [rest_got, x0],
        [shaped((half_r, 2 * width), F32), shaped((2, width, width))],
        after=[t1],
    )

    def x1_t23(meta, *refs):
        (near_two, far_two, diag, u, linked, x1), outs, whole = refs[:6], refs[6:-1], refs[-1]
        chip = chip_of(meta)
        x = jnp.zeros((half_r, width), F32)
        for m in range(chips):
            part = (near_two, far_two)[m // 2][(m % 2) * half_r : (m % 2 + 1) * half_r]
            x = x + dot(part, diag[at(chip ^ m, lanes)])
        x = x.astype(BF16)
        x1[...] = x
        for i in range(2):
            cols = slice(i * width, (i + 1) * width)
            whole[:, cols] = u[:, cols] - dot(x, linked[i])
        for m, out in enumerate(outs):
            out[...] = whole[at(chip ^ m, part_r)].astype(BF16)

    pair = Picked(diag_pair, (None, width, width), lambda i, *meta: (lax.div(leaf_of(meta), 2), 0, 0))
    strip = shaped((part_r, 2 * width))
    x1, *strips = run(
        x1_t23,
        [m1, m1_far, pair, u, linked],
        [rows_half] + [strip] * chips,
        [pltpu.VMEM((half_r, 2 * width), F32)],
    )
    strips[1:] = [swap(piece, "row", step) for piece, step in zip(strips[1:], steps_up)]
    x01_other = [swap(x, "row", 1) for x in (x0, x1)]

    ways = ((1, 2), (2, 1))

    def leaf_tile(array, level):
        if level is None:
            return Picked(array, (None, height, width), lambda i, *meta: (leaf_of(meta) ^ i, 0, 0))
        return Picked(
            array, (None, None, width, width), lambda i, *meta: (level, leaf_of(meta) ^ i, 0, 0)
        )

    def update01(meta, b, pa, pb, x0, x1, x0_other, x1_other, *refs):
        sends, kept, whole = refs[:2], refs[2:4], refs[4]
        step = pl.program_id(0)
        core = core_of(meta)
        a = leaf_of(meta) ^ step

        @pl.when(step == 0)
        def _():
            for i, (mine, other) in enumerate(((x0, x0_other), (x1, x1_other))):
                whole[i, at(core, half_r)] = mine[...]
                whole[i, at(1 - core, half_r)] = other[...]

        value = b[...].astype(F32)
        for i, p in enumerate((pa, pb)):
            value = value - dot(whole[i], p[...] * keep(live(meta, i, a)))
        for half, (one, two) in enumerate(ways):
            part = value[half * half_r : (half + 1) * half_r]
            for i, m in enumerate((one, one ^ two)):
                @pl.when(step == m)
                def _(half=half, i=i, part=part):
                    sends[half][i] = part.astype(BF16)
            for i, m in enumerate((0, two)):
                @pl.when(step == m)
                def _(half=half, i=i, part=part):
                    kept[half][i] = part

    share_pair = (2, half_r, width)
    share_send0, share_send1, share_kept0, share_kept1 = run(
        update01,
        [leaf_tile(right, None), leaf_tile(panels, 0), leaf_tile(panels, 1), x0, x1] + x01_other,
        [shaped(share_pair)] * 2 + [shaped(share_pair, F32)] * 2,
        [pltpu.VMEM((2, height, width), BF16)],
        steps=n_leaf,
    )
    share_got = [swap(share_send0, "leaf", ways[0][0]), swap(share_send1, "leaf", ways[1][0])]

    def share_join(meta, kept0, kept1, got0, got1, out0, out1):
        for kept, got, out in ((kept0, got0, out0), (kept1, got1, out1)):
            out[...] = (kept[1] + got[1].astype(F32)).astype(BF16)

    share_sent = run(
        share_join, [share_kept0, share_kept1] + share_got, [shaped((half_r, width))] * 2
    )
    share_far = [swap(sent, "leaf", way[1]) for sent, way in zip(share_sent, ways)]

    def t23_sum(meta, *refs):
        value = refs[0][...]
        for ref in refs[1:-1]:
            value = value + ref[...]
        refs[-1][...] = value

    t23 = spread(run(t23_sum, strips, strip, after=[share_send0]))
    t23 = t23.astype(F32) + swap(t23, "leaf", 1).astype(F32)
    t23_far = swap(t23, "leaf", 2)

    def m23_sum(meta, a, b, out):
        out[...] = (a[...] + b[...]).astype(BF16)

    m23 = run(
        m23_sum,
        [t23, t23_far],
        strip,
        after=[p23_half, *share_sent, *panel_far],
    )
    m23_parts = [m23] + [swap(m23, "row", step) for step in steps_up]

    def leaf_sums(meta, pa, pb, ga, gb, fa, fb, k0, k1, g0, g1, f0, f1, panel_out, share_out):
        for i, (p, got, far) in enumerate(((pa, ga, fa), (pb, gb, fb))):
            value = panel_value(meta, p, 2 + i, 0).astype(F32)
            panel_out[i] = (value + got[0].astype(F32) + far[...].astype(F32)).astype(BF16)
        for i, (kept, got, far) in enumerate(((k0, g0, f0), (k1, g1, f1))):
            value = kept[0] + got[0].astype(F32) + far[...].astype(F32)
            share_out[i * half_r : (i + 1) * half_r] = value

    panel_sum, share_sum = run(
        leaf_sums,
        [panel_of(2, 0), panel_of(3, 0)]
        + panel_got
        + panel_far
        + [share_kept0, share_kept1]
        + share_got
        + share_far,
        [shaped((2, width, width)), shaped((height, width), F32)],
    )

    def x2_x3(meta, *refs):
        parts, (diag, p, p_other, out, whole, tile23) = refs[:chips], refs[chips:]
        chip, core = chip_of(meta), core_of(meta)
        for m, part in enumerate(parts):
            whole[at(chip ^ m, part_r)] = part[...]
        tile23[at(core, half_w)] = p[...]
        tile23[at(1 - core, half_w)] = p_other[...]
        x = dot(whole[:, :width], diag[0]).astype(BF16)
        out[0] = x
        merged = whole[:, width:].astype(F32) - dot(x, tile23[...])
        out[1] = dot(merged.astype(BF16), diag[1]).astype(BF16)

    x23 = run(
        x2_x3,
        m23_parts + [diag_root, p23_half, p23_other],
        shaped((2, half_r, width)),
        [pltpu.VMEM((half_r, 2 * width), BF16), pltpu.VMEM((width, width), BF16)],
        after=[share_sum],
    )
    x23_other = swap(x23, "row", 1)

    def final(meta, x0, x1, x0_other, x1_other, x23, x23_other, panel, share, solved, out):
        core = core_of(meta)
        mine, other = at(core, half_r), at(1 - core, half_r)
        for i, (a, b) in enumerate(((x0, x0_other), (x1, x1_other))):
            solved[i, mine] = a[...]
            solved[i, other] = b[...]
        value = share[...]
        for i in range(2):
            solved[2 + i, mine] = x23[i]
            solved[2 + i, other] = x23_other[i]
            value = value - dot(solved[2 + i], panel[i])
        value = value.astype(BF16)
        for i in range(n_leaf):
            out[i] = value

    solved, done = run(
        final,
        [x0, x1] + x01_other + [x23, x23_other, panel_sum, share_sum],
        [shaped((levels, height, width)), shaped((n_leaf, height, width))],
    )
    updated = lax.all_to_all(done, "leaf", 0, 0, tiled=True)
    return solved[:, None], updated


def solution(mesh):
    return jax.shard_map(
        on_device,
        mesh=mesh,
        in_specs=(
            P("leaf", "row", None, None),
            P(None, "leaf", "row", None, None),
            P(None, "leaf", "row"),
            P("leaf", None, None),
            P(),
            P(),
            P(),
        ),
        out_specs=(P(None, "leaf", None, None), P("row", None, None)),
        check_vma=False,
    )
```

```python
import jax
import jax.numpy as jnp
from jax import lax
from jax.experimental import pallas as pl
from jax.experimental.pallas import tpu as pltpu
from jax.sharding import PartitionSpec as P

F32 = jnp.float32
BF16 = jnp.bfloat16
CORES = 2


def swap(block, axis, bits):
    return lax.ppermute(block, axis, [(i, i ^ bits) for i in range(lax.axis_size(axis))])


def dot(a, b):
    return jnp.dot(a, b, preferred_element_type=F32)


def shaped(shape, dtype=BF16):
    return jax.ShapeDtypeStruct(tuple(shape), dtype)


class Picked:
    def __init__(self, array, block, index):
        self.array, self.block, self.index = array, block, index


class InHbm:
    def __init__(self, array):
        self.array = array


def on_device(right_side, panels, tile_counts, diag_leaf, diag_pair, diag_root, sup_rows):
    right, panels, counts = right_side[0], panels[:, 0], tile_counts[:, 0]
    levels, here, width, _ = panels.shape
    n_row, n_leaf = lax.axis_size("row"), lax.axis_size("leaf")
    chips = min(n_row // CORES, 4)
    outer = [1 << b for b in range(n_row.bit_length()) if CORES * chips <= 1 << b < n_row]
    height = right.shape[1]
    half_r, half_w = height // CORES, width // CORES
    part_r, part_w = half_r // chips, width // chips

    def row_of(meta):
        return lax.axis_index("row")

    def leaf_of(meta):
        return lax.axis_index("leaf")

    def core_of(meta):
        return row_of(meta) & (CORES - 1)

    def chip_of(meta):
        return lax.div(row_of(meta), CORES) & (chips - 1)

    def spot(meta, level):
        return lax.rem(meta[0][level], here)

    def owns(meta, level):
        return lax.div(meta[0][level], here) == row_of(meta)

    def live(meta, level, a):
        kept = meta[1][level, a]
        for m in range(level + 1):
            kept = jnp.where(row_of(meta) * here + a == meta[0][m], 0, kept)
        return kept

    def live_owned(meta, of, level):
        return jnp.where(owns(meta, level), live(meta, of, spot(meta, level)), 0)

    def keep(limit):
        ids = lax.broadcasted_iota(jnp.int32, (1, width), 1)
        return (ids < limit).astype(F32).astype(BF16)

    def side(level, other):
        return Picked(
            right,
            (None, half_r, width),
            lambda i, *meta: (spot(meta, level), core_of(meta) ^ other, 0),
        )

    def side_value(meta, ref, level):
        return ref[...] * keep(jnp.where(owns(meta, level), width, 0))

    def tile(of, level, other=None):
        if other is None:
            return Picked(
                panels, (None, None, width, width), lambda i, *meta: (of, spot(meta, level), 0, 0)
            )
        return Picked(
            panels,
            (None, None, half_w, width),
            lambda i, *meta: (of, spot(meta, level), core_of(meta) ^ other, 0),
        )

    def tile_value(meta, ref, of, level):
        return ref[...] * keep(live_owned(meta, of, level))

    def run(body, operands, outs, scratch=(), steps=1, after=(), limit=32):
        arrays, specs, moved = [], [], 0
        for operand in operands:
            if isinstance(operand, InHbm):
                arrays.append(operand.array)
                specs.append(pl.BlockSpec(memory_space=pltpu.HBM))
                continue
            if not isinstance(operand, Picked):
                zeros = (0,) * operand.ndim
                operand = Picked(operand, operand.shape, lambda i, sup, live_counts, zeros=zeros: zeros)
            arrays.append(operand.array)
            specs.append(pl.BlockSpec(operand.block, operand.index))
            size = operand.array.dtype.itemsize
            for n in operand.block:
                size *= n or 1
            moved += size * steps
        taken = len(arrays)
        arrays += list(after)
        specs += [pl.BlockSpec(memory_space=pl.ANY)] * len(after)

        def kernel(sup, live_counts, *refs):
            body((sup, live_counts), *refs[:taken], *refs[taken + len(after) :])

        single = not isinstance(outs, (list, tuple))
        listed = [outs] if single else list(outs)
        out_specs = [
            pl.BlockSpec(out.shape, lambda i, sup, live_counts, zeros=(0,) * len(out.shape): zeros)
            for out in listed
        ]
        moved += sum(out.size * out.dtype.itemsize for out in listed)
        results = pl.pallas_call(
            kernel,
            grid_spec=pltpu.PrefetchScalarGridSpec(
                num_scalar_prefetch=2,
                grid=(steps,),
                in_specs=specs,
                out_specs=out_specs,
                scratch_shapes=list(scratch),
            ),
            out_shape=listed,
            name=body.__name__,
            compiler_params=pltpu.CompilerParams(vmem_limit_bytes=limit * 1024 * 1024),
            cost_estimate=pl.CostEstimate(flops=0, bytes_accessed=moved, transcendentals=0),
        )(sup_rows, counts, *arrays)
        return results[0] if single else list(results)

    def spread(block):
        for bits in outer:
            block = block + swap(block, "row", bits)
        return block

    steps_up = [CORES * m for m in range(1, chips)]
    rows_half = shaped((half_r, width))
    lanes = part_w
    blocks = width // lanes

    def at(index, size):
        return pl.ds(pl.multiple_of(index * size, size), size)

    first_rows = 2 * half_r + 2 * half_w

    def first_send(meta, sides, tiles, send, kept, sem):
        core = core_of(meta)
        copies, start = [], 0
        for source, level in ((None, 0), (None, 1), (0, 1), (2, 3)):
            size = half_r if source is None else half_w
            whole = sides if source is None else tiles.at[source]
            for out, side_of in ((send, 1 - core), (kept, core)):
                copies.append(
                    pltpu.make_async_copy(
                        whole.at[spot(meta, level), at(side_of, size)],
                        out.at[start : start + size],
                        sem.at[len(copies)],
                    )
                )
            start += size
        for copy in copies:
            copy.start()
        for copy in copies:
            copy.wait()
        for out in (send, kept):
            for level in range(2):
                rows = slice(level * half_r, (level + 1) * half_r)
                out[rows] = out[rows] * keep(jnp.where(owns(meta, level), width, 0))
            for i, (of, level) in enumerate(((0, 1), (2, 3))):
                rows = slice(2 * half_r + i * half_w, 2 * half_r + (i + 1) * half_w)
                out[rows] = out[rows] * keep(live_owned(meta, of, level))

    first_shape = shaped((first_rows, width))
    first_out, first_kept = run(
        first_send,
        [InHbm(right), InHbm(panels)],
        [first_shape, first_shape],
        [pltpu.SemaphoreType.DMA((8,))],
        limit=60,
    )
    first_got = swap(first_out, "row", 1)

    b0_rows, column_rows = blocks * half_r, half_r + half_w
    near, far = (CORES, 2 * CORES)

    def first_split(meta, own, got, send, kept, p23_send, p23_kept, whole):
        whole[...] = own[...] + got[...]
        for i in range(blocks):
            send[i * half_r : (i + 1) * half_r] = whole[:half_r, i * lanes : (i + 1) * lanes]
        kept[:b0_rows] = send[:b0_rows]
        chip = chip_of(meta)
        for i, (mine, other) in enumerate(((0, 1), (2, 3))):
            rows = slice(b0_rows + i * column_rows, b0_rows + (i + 1) * column_rows)
            source = slice(half_r, half_r + column_rows)
            send[rows] = whole[source, at(chip ^ other, lanes)]
            kept[rows] = whole[source, at(chip ^ mine, lanes)]
            rows = slice(i * half_w, (i + 1) * half_w)
            source = slice(half_r + column_rows, first_rows)
            p23_send[rows] = whole[source, at(chip ^ other, lanes)]
            p23_kept[rows] = whole[source, at(chip ^ mine, lanes)]

    near_shape, p23_pair = (
        shaped((b0_rows + 2 * column_rows, lanes)),
        shaped((2 * half_w, lanes)),
    )
    near_send, near_kept, p23_send, p23_kept = run(
        first_split,
        [first_kept, first_got],
        [near_shape, near_shape, p23_pair, p23_pair],
        [pltpu.VMEM((first_rows, width), BF16)],
    )
    near_got = swap(spread(near_send), "row", near)
    near_kept = spread(near_kept)
    p23_got = swap(spread(p23_send), "row", near)
    p23_kept = spread(p23_kept)

    def panel_of(level, m):
        return Picked(
            panels,
            (None, None, width, width),
            lambda i, *meta: (level, leaf_of(meta) ^ m, 0, 0),
        )

    def panel_value(meta, ref, level, m):
        return ref[...] * keep(live(meta, level, leaf_of(meta) ^ m))

    orders = ((2, 1, 2), (3, 2, 1))
    panel_got, first_sent = [], []
    for level, one, two in orders:
        def panel_send(meta, pa, pb, out, level=level, one=one, two=two):
            out[0] = panel_value(meta, pa, level, one)
            out[1] = panel_value(meta, pb, level, one ^ two)

        sent = run(
            panel_send,
            [panel_of(level, one), panel_of(level, one ^ two)],
            shaped((2, width, width)),
            after=[near_send],
        )
        first_sent.append(sent)
        panel_got.append(swap(sent, "leaf", one))

    def first_join(meta, kept, got, send, own):
        send[:b0_rows] = kept[:b0_rows] + got[:b0_rows]
        middle = b0_rows + column_rows
        own[...] = kept[b0_rows:middle] + got[b0_rows:middle]
        send[b0_rows:] = kept[middle:] + got[middle:]

    far_send, columns_own = run(
        first_join,
        [near_kept, near_got],
        [shaped((b0_rows + column_rows, lanes)), shaped((column_rows, lanes))],
        after=first_sent,
    )
    far_got = swap(far_send, "row", far)

    def p23_join(meta, kept, got, send, own):
        own[...] = kept[:half_w] + got[:half_w]
        send[...] = kept[half_w:] + got[half_w:]

    p23_block = shaped((half_w, lanes))
    p23_send, p23_own = run(
        p23_join, [p23_kept, p23_got], [p23_block, p23_block], after=[far_send]
    )
    p23_far = swap(p23_send, "row", far)

    rest_got, linked_got = [], []
    for level in (2, 3):
        def rest_send(meta, b, p0, p1, out, linked_out, level=level):
            out[:half_r] = side_value(meta, b, level)
            out[half_r:] = tile_value(meta, p0, 0, level)
            linked_out[...] = tile_value(meta, p1, 1, level)

        rest_sent, linked_sent = run(
            rest_send,
            [side(level, 1), tile(0, level), tile(1, level)],
            [shaped((half_r + width, width)), shaped((width, width))],
            after=[near_send],
        )
        rest_got.append(swap(rest_sent, "row", 1))
        linked_got.append(swap(linked_sent, "row", 1))

    def solve0(meta, sent, got, own, diag, x0, p, b):
        x = jnp.zeros((half_r, width), F32)
        for i in range(blocks):
            rows = slice(i * half_r, (i + 1) * half_r)
            x = x + dot(sent[rows] + got[rows], diag[0, i * lanes : (i + 1) * lanes])
        x0[...] = x.astype(BF16)
        b[...] = own[:half_r] + got[b0_rows : b0_rows + half_r]
        p[...] = own[half_r:] + got[b0_rows + half_r :]

    x0, p01, b1 = run(
        solve0,
        [far_send, far_got, columns_own, diag_leaf],
        [rows_half, shaped((half_w, lanes)), shaped((half_r, lanes))],
        after=[p23_send],
    )
    p01_other = swap(p01, "row", 1)

    def term1(meta, x0, p, p_other, b, t1, whole):
        core = core_of(meta)
        whole[at(core, half_w)] = p[...]
        whole[at(1 - core, half_w)] = p_other[...]
        t1[...] = b[...].astype(F32) - dot(x0[...], whole[...])

    t1 = run(
        term1,
        [x0, p01, p01_other, b1],
        shaped((half_r, lanes), F32),
        [pltpu.VMEM((width, lanes), BF16)],
        after=[p23_far],
    )
    panel_far, panel_sent = [], []
    for (level, one, two), got in zip(orders, panel_got):
        def panel_join(meta, p, got, out, level=level, two=two):
            value = panel_value(meta, p, level, two).astype(F32) + got[1].astype(F32)
            out[...] = value.astype(BF16)

        sent = run(
            panel_join, [panel_of(level, two), got], shaped((width, width)), after=[t1]
        )
        panel_sent.append(sent)
        panel_far.append(swap(sent, "leaf", two))

    p23 = p23_own + p23_far
    p23 = (p23.astype(F32) + swap(p23, "leaf", 1).astype(F32)).astype(BF16)
    p23_turned = swap(p23, "leaf", 2)

    def m1_sum(meta, a, b, out):
        out[...] = (a[...] + b[...]).astype(BF16)

    m1 = run(m1_sum, [t1, swap(t1, "leaf", 1)], shaped((half_r, lanes)))
    m1 = jnp.concatenate([m1, swap(m1, "row", near)])
    m1_far = swap(m1, "row", far)
    p23 = (p23.astype(F32) + p23_turned.astype(F32)).astype(BF16)
    p23_next = swap(p23, "row", near)

    def early(meta, *refs):
        x0, us = refs[6], refs[7:]
        for i in range(2):
            b, p0, got = refs[3 * i : 3 * i + 3]
            value = (side_value(meta, b, 2 + i) + got[:half_r]).astype(F32)
            us[i][...] = value - dot(x0[...], tile_value(meta, p0, 0, 2 + i) + got[half_r:])

    us = run(
        early,
        [side(2, 0), tile(0, 2), rest_got[0], side(3, 0), tile(0, 3), rest_got[1], x0],
        [shaped((half_r, width), F32)] * 2,
        after=[t1],
    )

    def x1_t23(meta, *refs):
        (near_two, far_two, diag), us, ps, got = refs[:3], refs[3:5], refs[5:7], refs[7:9]
        x1, outs, whole = refs[9], refs[10:-1], refs[-1]
        chip = chip_of(meta)
        x = jnp.zeros((half_r, width), F32)
        for m in range(chips):
            part = (near_two, far_two)[m // 2][(m % 2) * half_r : (m % 2 + 1) * half_r]
            x = x + dot(part, diag[at(chip ^ m, lanes)])
        x = x.astype(BF16)
        x1[...] = x
        for i in range(2):
            cols = slice(i * width, (i + 1) * width)
            whole[:, cols] = us[i][...] - dot(x, tile_value(meta, ps[i], 1, 2 + i) + got[i][...])
        for m, out in enumerate(outs):
            out[...] = whole[at(chip ^ m, part_r)].astype(BF16)

    pair = Picked(diag_pair, (None, width, width), lambda i, *meta: (lax.div(leaf_of(meta), 2), 0, 0))
    strip = shaped((part_r, 2 * width))
    x1, *strips = run(
        x1_t23,
        [m1, m1_far, pair] + us + [tile(1, 2), tile(1, 3)] + linked_got,
        [rows_half] + [strip] * chips,
        [pltpu.VMEM((half_r, 2 * width), F32)],
        after=panel_sent,
    )
    strips[1:] = [swap(piece, "row", step) for piece, step in zip(strips[1:], steps_up)]
    x01_other = [swap(x, "row", 1) for x in (x0, x1)]

    ways = ((1, 2), (2, 1))

    def leaf_tile(array, level):
        if level is None:
            return Picked(array, (None, height, width), lambda i, *meta: (leaf_of(meta) ^ i, 0, 0))
        return Picked(
            array, (None, None, width, width), lambda i, *meta: (level, leaf_of(meta) ^ i, 0, 0)
        )

    def update01(meta, b, pa, pb, x0, x1, x0_other, x1_other, *refs):
        sends, kept, whole = refs[:2], refs[2:4], refs[4]
        step = pl.program_id(0)
        core = core_of(meta)
        a = leaf_of(meta) ^ step

        @pl.when(step == 0)
        def _():
            for i, (mine, other) in enumerate(((x0, x0_other), (x1, x1_other))):
                whole[i, at(core, half_r)] = mine[...]
                whole[i, at(1 - core, half_r)] = other[...]

        value = b[...].astype(F32)
        for i, p in enumerate((pa, pb)):
            value = value - dot(whole[i], p[...] * keep(live(meta, i, a)))
        for half, (one, two) in enumerate(ways):
            part = value[half * half_r : (half + 1) * half_r]
            for i, m in enumerate((one, one ^ two)):
                @pl.when(step == m)
                def _(half=half, i=i, part=part):
                    sends[half][i] = part.astype(BF16)
            for i, m in enumerate((0, two)):
                @pl.when(step == m)
                def _(half=half, i=i, part=part):
                    kept[half][i] = part

    share_pair = (2, half_r, width)
    share_send0, share_send1, share_kept0, share_kept1 = run(
        update01,
        [leaf_tile(right, None), leaf_tile(panels, 0), leaf_tile(panels, 1), x0, x1] + x01_other,
        [shaped(share_pair)] * 2 + [shaped(share_pair, F32)] * 2,
        [pltpu.VMEM((2, height, width), BF16)],
        steps=n_leaf,
    )
    share_got = [swap(share_send0, "leaf", ways[0][0]), swap(share_send1, "leaf", ways[1][0])]

    def share_join(meta, kept0, kept1, got0, got1, out0, out1):
        for kept, got, out in ((kept0, got0, out0), (kept1, got1, out1)):
            out[...] = (kept[1] + got[1].astype(F32)).astype(BF16)

    share_sent = run(
        share_join, [share_kept0, share_kept1] + share_got, [shaped((half_r, width))] * 2
    )
    share_far = [swap(sent, "leaf", way[1]) for sent, way in zip(share_sent, ways)]

    def t23_sum(meta, *refs):
        value = refs[0][...]
        for ref in refs[1:-1]:
            value = value + ref[...]
        refs[-1][...] = value

    t23 = spread(run(t23_sum, strips, strip, after=[share_send0]))
    def p23_stack(meta, a, b, out):
        out[:half_w] = a[...]
        out[half_w:] = b[...]

    p23 = run(p23_stack, [p23, p23_next], p23_pair, after=[t23])
    p23_far = swap(p23, "row", far)

    def p23_place(meta, near_two, far_two, out):
        for m in range(chips):
            source = (near_two, far_two)[m // 2]
            rows = slice((m % 2) * half_w, (m % 2 + 1) * half_w)
            out[:, at(chip_of(meta) ^ m, lanes)] = source[rows]

    p23_half = run(p23_place, [p23, p23_far], shaped((half_w, width)))
    p23_other = swap(p23_half, "row", 1)

    t23 = t23.astype(F32) + swap(t23, "leaf", 1).astype(F32)
    t23_far = swap(t23, "leaf", 2)

    def m23_sum(meta, a, b, out):
        out[...] = (a[...] + b[...]).astype(BF16)

    m23 = run(
        m23_sum,
        [t23, t23_far],
        strip,
        after=[p23_half, *panel_far],
    )
    m23_parts = [m23] + [swap(m23, "row", step) for step in steps_up]

    def leaf_sums(meta, pa, pb, ga, gb, fa, fb, k0, k1, g0, g1, f0, f1, panel_out, share_out):
        for i, (p, got, far) in enumerate(((pa, ga, fa), (pb, gb, fb))):
            value = panel_value(meta, p, 2 + i, 0).astype(F32)
            panel_out[i] = (value + got[0].astype(F32) + far[...].astype(F32)).astype(BF16)
        for i, (kept, got, far) in enumerate(((k0, g0, f0), (k1, g1, f1))):
            value = kept[0] + got[0].astype(F32) + far[...].astype(F32)
            share_out[i * half_r : (i + 1) * half_r] = value

    panel_sum, share_sum = run(
        leaf_sums,
        [panel_of(2, 0), panel_of(3, 0)]
        + panel_got
        + panel_far
        + [share_kept0, share_kept1]
        + share_got
        + share_far,
        [shaped((2, width, width)), shaped((height, width), F32)],
    )

    def x2_x3(meta, *refs):
        parts, (diag, p, p_other, out, whole, tile23) = refs[:chips], refs[chips:]
        chip, core = chip_of(meta), core_of(meta)
        for m, part in enumerate(parts):
            whole[at(chip ^ m, part_r)] = part[...]
        tile23[at(core, half_w)] = p[...]
        tile23[at(1 - core, half_w)] = p_other[...]
        x = dot(whole[:, :width], diag[0]).astype(BF16)
        out[0] = x
        merged = whole[:, width:].astype(F32) - dot(x, tile23[...])
        out[1] = dot(merged.astype(BF16), diag[1]).astype(BF16)

    x23 = run(
        x2_x3,
        m23_parts + [diag_root, p23_half, p23_other],
        shaped((2, half_r, width)),
        [pltpu.VMEM((half_r, 2 * width), BF16), pltpu.VMEM((width, width), BF16)],
        after=[share_sum],
    )
    x23_other = swap(x23, "row", 1)

    def final(meta, x23, x23_other, panel, share, top, bottom, whole):
        core = core_of(meta)
        value = share[...]
        for i in range(2):
            whole[i, at(core, half_r)] = x23[i]
            whole[i, at(1 - core, half_r)] = x23_other[i]
            value = value - dot(whole[i], panel[i])
        top[...] = value[:half_r].astype(BF16)
        bottom[...] = value[half_r:].astype(BF16)

    top, bottom = run(
        final,
        [x23, x23_other, panel_sum, share_sum],
        [rows_half, rows_half],
        [pltpu.VMEM((2, height, width), BF16)],
    )

    def write_solved(meta, x0, x1, x0_other, x1_other, x23, x23_other, out):
        core = core_of(meta)
        mine, other = at(core, half_r), at(1 - core, half_r)
        for i, (a, b) in enumerate(((x0, x0_other), (x1, x1_other))):
            out[i, mine] = a[...]
            out[i, other] = b[...]
        for i in range(2):
            out[2 + i, mine] = x23[i]
            out[2 + i, other] = x23_other[i]

    solved = run(
        write_solved,
        [x0, x1] + x01_other + [x23, x23_other],
        shaped((levels, height, width)),
        after=[top],
    )

    top_1, bottom_2 = swap(top, "leaf", 1), swap(bottom, "leaf", 2)
    bottom_1, top_2 = swap(bottom, "leaf", 1), swap(top, "leaf", 2)
    top_3, bottom_3 = swap(top_1, "leaf", 2), swap(bottom_2, "leaf", 1)

    def write_updated(meta, *refs):
        parts, out = refs[:-1], refs[-1]
        for m in range(n_leaf):
            for half in range(2):
                rows = slice(half * half_r, (half + 1) * half_r)
                out[leaf_of(meta) ^ m, rows] = parts[2 * m + half][...]

    updated = run(
        write_updated,
        [top, bottom, top_1, bottom_1, top_2, bottom_2, top_3, bottom_3],
        shaped((n_leaf, height, width)),
        after=[solved],
    )
    return solved[:, None], updated


def solution(mesh):
    return jax.shard_map(
        on_device,
        mesh=mesh,
        in_specs=(
            P("leaf", "row", None, None),
            P(None, "leaf", "row", None, None),
            P(None, "leaf", "row"),
            P("leaf", None, None),
            P(),
            P(),
            P(),
        ),
        out_specs=(P(None, "leaf", None, None), P("row", None, None)),
        check_vma=False,
    )
```

```python
import jax
import jax.numpy as jnp
from jax import lax
from jax.experimental import pallas as pl
from jax.experimental.pallas import tpu as pltpu
from jax.sharding import PartitionSpec as P

F32 = jnp.float32
BF16 = jnp.bfloat16
CORES = 2


def swap(block, axis, bits):
    return lax.ppermute(block, axis, [(i, i ^ bits) for i in range(lax.axis_size(axis))])


def dot(a, b):
    return jnp.dot(a, b, preferred_element_type=F32)


def shaped(shape, dtype=BF16):
    return jax.ShapeDtypeStruct(tuple(shape), dtype)


class Picked:
    def __init__(self, array, block, index):
        self.array, self.block, self.index = array, block, index


class InHbm:
    def __init__(self, array):
        self.array = array


def on_device(right_side, panels, tile_counts, diag_leaf, diag_pair, diag_root, sup_rows):
    right, panels, counts = right_side[0], panels[:, 0], tile_counts[:, 0]
    levels, here, width, _ = panels.shape
    n_row, n_leaf = lax.axis_size("row"), lax.axis_size("leaf")
    chips = min(n_row // CORES, 4)
    outer = [1 << b for b in range(n_row.bit_length()) if CORES * chips <= 1 << b < n_row]
    height = right.shape[1]
    half_r, half_w = height // CORES, width // CORES
    part_r, part_w = half_r // chips, width // chips

    def row_of(meta):
        return lax.axis_index("row")

    def leaf_of(meta):
        return lax.axis_index("leaf")

    def core_of(meta):
        return row_of(meta) & (CORES - 1)

    def chip_of(meta):
        return lax.div(row_of(meta), CORES) & (chips - 1)

    def spot(meta, level):
        return lax.rem(meta[0][level], here)

    def owns(meta, level):
        return lax.div(meta[0][level], here) == row_of(meta)

    def live(meta, level, a):
        kept = meta[1][level, a]
        for m in range(level + 1):
            kept = jnp.where(row_of(meta) * here + a == meta[0][m], 0, kept)
        return kept

    def live_owned(meta, of, level):
        return jnp.where(owns(meta, level), live(meta, of, spot(meta, level)), 0)

    def keep(limit):
        ids = lax.broadcasted_iota(jnp.int32, (1, width), 1)
        return (ids < limit).astype(F32).astype(BF16)

    def side(level, other):
        return Picked(
            right,
            (None, half_r, width),
            lambda i, *meta: (spot(meta, level), core_of(meta) ^ other, 0),
        )

    def side_value(meta, ref, level):
        return ref[...] * keep(jnp.where(owns(meta, level), width, 0))

    def tile(of, level, other=None):
        if other is None:
            return Picked(
                panels, (None, None, width, width), lambda i, *meta: (of, spot(meta, level), 0, 0)
            )
        return Picked(
            panels,
            (None, None, half_w, width),
            lambda i, *meta: (of, spot(meta, level), core_of(meta) ^ other, 0),
        )

    def tile_value(meta, ref, of, level):
        return ref[...] * keep(live_owned(meta, of, level))

    def run(body, operands, outs, scratch=(), steps=1, after=(), limit=40):
        arrays, specs, moved = [], [], 0
        for operand in operands:
            if isinstance(operand, InHbm):
                arrays.append(operand.array)
                specs.append(pl.BlockSpec(memory_space=pltpu.HBM))
                continue
            if not isinstance(operand, Picked):
                zeros = (0,) * operand.ndim
                operand = Picked(operand, operand.shape, lambda i, sup, live_counts, zeros=zeros: zeros)
            arrays.append(operand.array)
            specs.append(pl.BlockSpec(operand.block, operand.index))
            size = operand.array.dtype.itemsize
            for n in operand.block:
                size *= n or 1
            moved += size * steps
        taken = len(arrays)
        arrays += list(after)
        specs += [pl.BlockSpec(memory_space=pl.ANY)] * len(after)

        def kernel(sup, live_counts, *refs):
            body((sup, live_counts), *refs[:taken], *refs[taken + len(after) :])

        single = not isinstance(outs, (list, tuple))
        listed = [outs] if single else list(outs)
        out_specs = [
            pl.BlockSpec(out.shape, lambda i, sup, live_counts, zeros=(0,) * len(out.shape): zeros)
            for out in listed
        ]
        moved += sum(out.size * out.dtype.itemsize for out in listed)
        results = pl.pallas_call(
            kernel,
            grid_spec=pltpu.PrefetchScalarGridSpec(
                num_scalar_prefetch=2,
                grid=(steps,),
                in_specs=specs,
                out_specs=out_specs,
                scratch_shapes=list(scratch),
            ),
            out_shape=listed,
            name=body.__name__,
            compiler_params=pltpu.CompilerParams(vmem_limit_bytes=limit * 1024 * 1024),
            cost_estimate=pl.CostEstimate(flops=0, bytes_accessed=moved, transcendentals=0),
        )(sup_rows, counts, *arrays)
        return results[0] if single else list(results)

    def spread(block):
        for bits in outer:
            block = block + swap(block, "row", bits)
        return block

    steps_up = [CORES * m for m in range(1, chips)]
    rows_half = shaped((half_r, width))
    lanes = part_w
    blocks = width // lanes

    def at(index, size):
        return pl.ds(pl.multiple_of(index * size, size), size)

    first_rows = 2 * half_r + 2 * half_w

    def first_send(meta, sides, tiles, send, kept, sem):
        core = core_of(meta)
        copies, start = [], 0
        for source, level in ((None, 0), (None, 1), (0, 1), (2, 3)):
            size = half_r if source is None else half_w
            whole = sides if source is None else tiles.at[source]
            for out, side_of in ((send, 1 - core), (kept, core)):
                copies.append(
                    pltpu.make_async_copy(
                        whole.at[spot(meta, level), at(side_of, size)],
                        out.at[start : start + size],
                        sem.at[len(copies)],
                    )
                )
            start += size
        for copy in copies:
            copy.start()
        for copy in copies:
            copy.wait()
        for out in (send, kept):
            for level in range(2):
                rows = slice(level * half_r, (level + 1) * half_r)
                out[rows] = out[rows] * keep(jnp.where(owns(meta, level), width, 0))
            for i, (of, level) in enumerate(((0, 1), (2, 3))):
                rows = slice(2 * half_r + i * half_w, 2 * half_r + (i + 1) * half_w)
                out[rows] = out[rows] * keep(live_owned(meta, of, level))

    first_shape = shaped((first_rows, width))
    first_out, first_kept = run(
        first_send,
        [InHbm(right), InHbm(panels)],
        [first_shape, first_shape],
        [pltpu.SemaphoreType.DMA((8,))],
        limit=60,
    )
    first_got = swap(first_out, "row", 1)

    b0_rows, column_rows = blocks * half_r, half_r + half_w
    near, far = (CORES, 2 * CORES)

    def first_split(meta, own, got, send, kept, p23_send, p23_kept, whole):
        whole[...] = own[...] + got[...]
        for i in range(blocks):
            send[i * half_r : (i + 1) * half_r] = whole[:half_r, i * lanes : (i + 1) * lanes]
        kept[:b0_rows] = send[:b0_rows]
        chip = chip_of(meta)
        for i, (mine, other) in enumerate(((0, 1), (2, 3))):
            rows = slice(b0_rows + i * column_rows, b0_rows + (i + 1) * column_rows)
            source = slice(half_r, half_r + column_rows)
            send[rows] = whole[source, at(chip ^ other, lanes)]
            kept[rows] = whole[source, at(chip ^ mine, lanes)]
            rows = slice(i * half_w, (i + 1) * half_w)
            source = slice(half_r + column_rows, first_rows)
            p23_send[rows] = whole[source, at(chip ^ other, lanes)]
            p23_kept[rows] = whole[source, at(chip ^ mine, lanes)]

    near_shape, p23_pair = (
        shaped((b0_rows + 2 * column_rows, lanes)),
        shaped((2 * half_w, lanes)),
    )
    near_send, near_kept, p23_send, p23_kept = run(
        first_split,
        [first_kept, first_got],
        [near_shape, near_shape, p23_pair, p23_pair],
        [pltpu.VMEM((first_rows, width), BF16)],
    )
    near_got = swap(spread(near_send), "row", near)
    near_kept = spread(near_kept)
    p23_got = swap(spread(p23_send), "row", near)
    p23_kept = spread(p23_kept)

    def panel_of(level, m):
        return Picked(
            panels,
            (None, None, width, width),
            lambda i, *meta: (level, leaf_of(meta) ^ m, 0, 0),
        )

    def panel_value(meta, ref, level, m):
        return ref[...] * keep(live(meta, level, leaf_of(meta) ^ m))

    orders = ((2, 1, 2), (3, 2, 1))
    panel_got, first_sent = [], []
    for level, one, two in orders:
        def panel_send(meta, pa, pb, out, level=level, one=one, two=two):
            out[0] = panel_value(meta, pa, level, one)
            out[1] = panel_value(meta, pb, level, one ^ two)

        sent = run(
            panel_send,
            [panel_of(level, one), panel_of(level, one ^ two)],
            shaped((2, width, width)),
            after=[near_send],
        )
        first_sent.append(sent)
        panel_got.append(swap(sent, "leaf", one))

    def first_join(meta, kept, got, send, own):
        send[:b0_rows] = kept[:b0_rows] + got[:b0_rows]
        middle = b0_rows + column_rows
        own[...] = kept[b0_rows:middle] + got[b0_rows:middle]
        send[b0_rows:] = kept[middle:] + got[middle:]

    far_send, columns_own = run(
        first_join,
        [near_kept, near_got],
        [shaped((b0_rows + column_rows, lanes)), shaped((column_rows, lanes))],
        after=[*first_sent],
    )
    far_got = swap(far_send, "row", far)

    def p23_join(meta, kept, got, send, own):
        own[...] = kept[:half_w] + got[:half_w]
        send[...] = kept[half_w:] + got[half_w:]

    p23_block = shaped((half_w, lanes))
    p23_send, p23_own = run(
        p23_join, [p23_kept, p23_got], [p23_block, p23_block], after=[far_send]
    )
    p23_far = swap(p23_send, "row", far)

    rest_got, linked_got = [], []
    for level in (2, 3):
        def rest_send(meta, b, p0, p1, out, linked_out, level=level):
            out[:half_r] = side_value(meta, b, level)
            out[half_r:] = tile_value(meta, p0, 0, level)
            linked_out[...] = tile_value(meta, p1, 1, level)

        rest_sent, linked_sent = run(
            rest_send,
            [side(level, 1), tile(0, level), tile(1, level)],
            [shaped((half_r + width, width)), shaped((width, width))],
            after=[near_send],
        )
        rest_got.append(swap(rest_sent, "row", 1))
        linked_got.append(swap(linked_sent, "row", 1))

    def solve0(meta, sent, got, own, diag, x0, p, b):
        x = jnp.zeros((half_r, width), F32)
        for i in range(blocks):
            rows = slice(i * half_r, (i + 1) * half_r)
            x = x + dot(sent[rows] + got[rows], diag[0, i * lanes : (i + 1) * lanes])
        x0[...] = x.astype(BF16)
        b[...] = own[:half_r] + got[b0_rows : b0_rows + half_r]
        p[...] = own[half_r:] + got[b0_rows + half_r :]

    x0, p01, b1 = run(
        solve0,
        [far_send, far_got, columns_own, diag_leaf],
        [rows_half, shaped((half_w, lanes)), shaped((half_r, lanes))],
        after=[p23_send],
    )
    x0_other = swap(x0, "row", 1)
    p01_other = swap(p01, "row", 1)

    def term1(meta, x0, p, p_other, b, t1, whole):
        core = core_of(meta)
        whole[at(core, half_w)] = p[...]
        whole[at(1 - core, half_w)] = p_other[...]
        t1[...] = b[...].astype(F32) - dot(x0[...], whole[...])

    t1 = run(
        term1,
        [x0, p01, p01_other, b1],
        shaped((half_r, lanes), F32),
        [pltpu.VMEM((width, lanes), BF16)],
        after=[p23_far],
    )
    panel_far, panel_sent = [], []
    for (level, one, two), got in zip(orders, panel_got):
        def panel_join(meta, p, got, out, level=level, two=two):
            value = panel_value(meta, p, level, two).astype(F32) + got[1].astype(F32)
            out[...] = value.astype(BF16)

        sent = run(
            panel_join, [panel_of(level, two), got], shaped((width, width)), after=[t1]
        )
        panel_sent.append(sent)
        panel_far.append(swap(sent, "leaf", two))

    p23 = p23_own + p23_far
    p23 = (p23.astype(F32) + swap(p23, "leaf", 1).astype(F32)).astype(BF16)
    p23_turned = swap(p23, "leaf", 2)

    def m1_sum(meta, a, b, out):
        out[...] = (a[...] + b[...]).astype(BF16)

    m1 = run(m1_sum, [t1, swap(t1, "leaf", 1)], shaped((half_r, lanes)), after=[])
    m1 = jnp.concatenate([m1, swap(m1, "row", near)])
    m1_far = swap(m1, "row", far)
    p23 = (p23.astype(F32) + p23_turned.astype(F32)).astype(BF16)
    p23_next = swap(p23, "row", near)

    def early(meta, *refs):
        x0, us = refs[6], refs[7:]
        for i in range(2):
            b, p0, got = refs[3 * i : 3 * i + 3]
            value = (side_value(meta, b, 2 + i) + got[:half_r]).astype(F32)
            us[i][...] = value - dot(x0[...], tile_value(meta, p0, 0, 2 + i) + got[half_r:])

    us = run(
        early,
        [side(2, 0), tile(0, 2), rest_got[0], side(3, 0), tile(0, 3), rest_got[1], x0],
        [shaped((half_r, width), F32)] * 2,
        after=[t1],
    )

    def x1_t23(meta, *refs):
        (near_two, far_two, diag), us, ps, got = refs[:3], refs[3:5], refs[5:7], refs[7:9]
        x1, outs, whole = refs[9], refs[10:-1], refs[-1]
        chip = chip_of(meta)
        x = jnp.zeros((half_r, width), F32)
        for m in range(chips):
            part = (near_two, far_two)[m // 2][(m % 2) * half_r : (m % 2 + 1) * half_r]
            x = x + dot(part, diag[at(chip ^ m, lanes)])
        x = x.astype(BF16)
        x1[...] = x
        for i in range(2):
            cols = slice(i * width, (i + 1) * width)
            whole[:, cols] = us[i][...] - dot(x, tile_value(meta, ps[i], 1, 2 + i) + got[i][...])
        for m, out in enumerate(outs):
            out[...] = whole[at(chip ^ m, part_r)].astype(BF16)

    pair = Picked(diag_pair, (None, width, width), lambda i, *meta: (lax.div(leaf_of(meta), 2), 0, 0))
    strip = shaped((part_r, 2 * width))
    x1, *strips = run(
        x1_t23,
        [m1, m1_far, pair] + us + [tile(1, 2), tile(1, 3)] + linked_got,
        [rows_half] + [strip] * chips,
        [pltpu.VMEM((half_r, 2 * width), F32)],
        after=[*panel_sent],
    )
    strips[1:] = [swap(piece, "row", step) for piece, step in zip(strips[1:], steps_up)]
    x01_other = [x0_other, swap(x1, "row", 1)]

    ways = ((1, 2), (2, 1))

    def leaf_tile(array, level):
        if level is None:
            return Picked(array, (None, height, width), lambda i, *meta: (leaf_of(meta) ^ i, 0, 0))
        return Picked(
            array, (None, None, width, width), lambda i, *meta: (level, leaf_of(meta) ^ i, 0, 0)
        )

    def update01(meta, b, pa, pb, x0, x1, x0_other, x1_other, *refs):
        sends, kept, whole = refs[:2], refs[2:4], refs[4]
        step = pl.program_id(0)
        core = core_of(meta)
        a = leaf_of(meta) ^ step

        @pl.when(step == 0)
        def _():
            for i, (mine, other) in enumerate(((x0, x0_other), (x1, x1_other))):
                whole[i, at(core, half_r)] = mine[...]
                whole[i, at(1 - core, half_r)] = other[...]

        value = b[...].astype(F32)
        for i, p in enumerate((pa, pb)):
            value = value - dot(whole[i], p[...] * keep(live(meta, i, a)))
        for half, (one, two) in enumerate(ways):
            part = value[half * half_r : (half + 1) * half_r]
            for i, m in enumerate((one, one ^ two)):
                @pl.when(step == m)
                def _(half=half, i=i, part=part):
                    sends[half][i] = part.astype(BF16)
            for i, m in enumerate((0, two)):
                @pl.when(step == m)
                def _(half=half, i=i, part=part):
                    kept[half][i] = part

    share_pair = (2, half_r, width)
    share_send0, share_send1, share_kept0, share_kept1 = run(
        update01,
        [leaf_tile(right, None), leaf_tile(panels, 0), leaf_tile(panels, 1), x0, x1] + x01_other,
        [shaped(share_pair)] * 2 + [shaped(share_pair, F32)] * 2,
        [pltpu.VMEM((2, height, width), BF16)],
        steps=n_leaf,
    )
    share_got = [swap(share_send0, "leaf", ways[0][0]), swap(share_send1, "leaf", ways[1][0])]

    def share_join(meta, kept0, kept1, got0, got1, out0, out1):
        for kept, got, out in ((kept0, got0, out0), (kept1, got1, out1)):
            out[...] = (kept[1] + got[1].astype(F32)).astype(BF16)

    share_sent = run(
        share_join, [share_kept0, share_kept1] + share_got, [shaped((half_r, width))] * 2
    )
    share_far = [swap(sent, "leaf", way[1]) for sent, way in zip(share_sent, ways)]

    def t23_sum(meta, *refs):
        value = refs[0][...]
        for ref in refs[1:-1]:
            value = value + ref[...]
        refs[-1][...] = value

    t23 = spread(run(t23_sum, strips, strip, after=[share_send0]))
    def p23_stack(meta, a, b, out):
        out[:half_w] = a[...]
        out[half_w:] = b[...]

    p23 = run(p23_stack, [p23, p23_next], p23_pair, after=[x1])
    p23_far = swap(p23, "row", far)

    def p23_place(meta, near_two, far_two, out):
        for m in range(chips):
            source = (near_two, far_two)[m // 2]
            rows = slice((m % 2) * half_w, (m % 2 + 1) * half_w)
            out[:, at(chip_of(meta) ^ m, lanes)] = source[rows]

    p23_half = run(p23_place, [p23, p23_far], shaped((half_w, width)))
    p23_other = swap(p23_half, "row", 1)

    t23 = t23.astype(F32) + swap(t23, "leaf", 1).astype(F32)
    t23_far = swap(t23, "leaf", 2)

    def m23_sum(meta, a, b, out):
        out[...] = (a[...] + b[...]).astype(BF16)

    m23 = run(
        m23_sum,
        [t23, t23_far],
        strip,
        after=[p23_half, *share_sent],
    )
    m23_parts = [m23] + [swap(m23, "row", step) for step in steps_up]

    def leaf_sums(meta, pa, pb, ga, gb, fa, fb, k0, k1, g0, g1, f0, f1, panel_out, share_out):
        for i, (p, got, far) in enumerate(((pa, ga, fa), (pb, gb, fb))):
            value = panel_value(meta, p, 2 + i, 0).astype(F32)
            panel_out[i] = (value + got[0].astype(F32) + far[...].astype(F32)).astype(BF16)
        for i, (kept, got, far) in enumerate(((k0, g0, f0), (k1, g1, f1))):
            value = kept[0] + got[0].astype(F32) + far[...].astype(F32)
            share_out[i * half_r : (i + 1) * half_r] = value

    panel_sum, share_sum = run(
        leaf_sums,
        [panel_of(2, 0), panel_of(3, 0)]
        + panel_got
        + panel_far
        + [share_kept0, share_kept1]
        + share_got
        + share_far,
        [shaped((2, width, width)), shaped((height, width), F32)],
    )

    def x2_x3(meta, *refs):
        parts, (diag, p, p_other, out, whole, tile23) = refs[:chips], refs[chips:]
        chip, core = chip_of(meta), core_of(meta)
        for m, part in enumerate(parts):
            whole[at(chip ^ m, part_r)] = part[...]
        tile23[at(core, half_w)] = p[...]
        tile23[at(1 - core, half_w)] = p_other[...]
        x = dot(whole[:, :width], diag[0]).astype(BF16)
        out[0] = x
        merged = whole[:, width:].astype(F32) - dot(x, tile23[...])
        out[1] = dot(merged.astype(BF16), diag[1]).astype(BF16)

    x23 = run(
        x2_x3,
        m23_parts + [diag_root, p23_half, p23_other],
        shaped((2, half_r, width)),
        [pltpu.VMEM((half_r, 2 * width), BF16), pltpu.VMEM((width, width), BF16)],
        after=[panel_sum],
    )
    x23_other = swap(x23, "row", 1)

    def final(meta, x23, x23_other, panel, share, top, bottom, whole):
        core = core_of(meta)
        value = share[...]
        for i in range(2):
            whole[i, at(core, half_r)] = x23[i]
            whole[i, at(1 - core, half_r)] = x23_other[i]
            value = value - dot(whole[i], panel[i])
        top[...] = value[:half_r].astype(BF16)
        bottom[...] = value[half_r:].astype(BF16)

    top, bottom = run(
        final,
        [x23, x23_other, panel_sum, share_sum],
        [rows_half, rows_half],
        [pltpu.VMEM((2, height, width), BF16)],
    )

    def write_solved(meta, x0, x1, x0_other, x1_other, x23, x23_other, out):
        core = core_of(meta)
        mine, other = at(core, half_r), at(1 - core, half_r)
        for i, (a, b) in enumerate(((x0, x0_other), (x1, x1_other))):
            out[i, mine] = a[...]
            out[i, other] = b[...]
        for i in range(2):
            out[2 + i, mine] = x23[i]
            out[2 + i, other] = x23_other[i]

    solved = run(
        write_solved,
        [x0, x1] + x01_other + [x23, x23_other],
        shaped((levels, height, width)),
        after=[top],
    )

    top_1, bottom_2 = swap(top, "leaf", 1), swap(bottom, "leaf", 2)
    bottom_1, top_2 = swap(bottom, "leaf", 1), swap(top, "leaf", 2)
    top_3, bottom_3 = swap(top_1, "leaf", 2), swap(bottom_2, "leaf", 1)

    def write_updated(meta, *refs):
        parts, out = refs[:-1], refs[-1]
        for m in range(n_leaf):
            for half in range(2):
                rows = slice(half * half_r, (half + 1) * half_r)
                out[leaf_of(meta) ^ m, rows] = parts[2 * m + half][...]

    updated = run(
        write_updated,
        [top, bottom, top_1, bottom_1, top_2, bottom_2, top_3, bottom_3],
        shaped((n_leaf, height, width)),
        after=[],
    )
    return solved[:, None], updated


def solution(mesh):
    return jax.shard_map(
        on_device,
        mesh=mesh,
        in_specs=(
            P("leaf", "row", None, None),
            P(None, "leaf", "row", None, None),
            P(None, "leaf", "row"),
            P("leaf", None, None),
            P(),
            P(),
            P(),
        ),
        out_specs=(P(None, "leaf", None, None), P("row", None, None)),
        check_vma=False,
    )
```

```python
import jax
import jax.numpy as jnp
from jax import lax
from jax.experimental import pallas as pl
from jax.experimental.pallas import tpu as pltpu
from jax.sharding import PartitionSpec as P

F32 = jnp.float32
BF16 = jnp.bfloat16
CORES = 2


def swap(block, axis, bits):
    return lax.ppermute(block, axis, [(i, i ^ bits) for i in range(lax.axis_size(axis))])


def dot(a, b):
    return jnp.dot(a, b, preferred_element_type=F32)


def shaped(shape, dtype=BF16):
    return jax.ShapeDtypeStruct(tuple(shape), dtype)


class Picked:
    def __init__(self, array, block, index):
        self.array, self.block, self.index = array, block, index


class InHbm:
    def __init__(self, array):
        self.array = array


def on_device(right_side, panels, tile_counts, diag_leaf, diag_pair, diag_root, sup_rows):
    right, panels, counts = right_side[0], panels[:, 0], tile_counts[:, 0]
    levels, here, width, _ = panels.shape
    n_row, n_leaf = lax.axis_size("row"), lax.axis_size("leaf")
    chips = min(n_row // CORES, 4)
    outer = [1 << b for b in range(n_row.bit_length()) if CORES * chips <= 1 << b < n_row]
    height = right.shape[1]
    half_r, half_w = height // CORES, width // CORES
    part_r, part_w = half_r // chips, width // chips

    def row_of(meta):
        return lax.axis_index("row")

    def leaf_of(meta):
        return lax.axis_index("leaf")

    def core_of(meta):
        return row_of(meta) & (CORES - 1)

    def chip_of(meta):
        return lax.div(row_of(meta), CORES) & (chips - 1)

    def spot(meta, level):
        return lax.rem(meta[0][level], here)

    def owns(meta, level):
        return lax.div(meta[0][level], here) == row_of(meta)

    def live(meta, level, a):
        kept = meta[1][level, a]
        for m in range(level + 1):
            kept = jnp.where(row_of(meta) * here + a == meta[0][m], 0, kept)
        return kept

    def live_owned(meta, of, level):
        return jnp.where(owns(meta, level), live(meta, of, spot(meta, level)), 0)

    def keep(limit):
        ids = lax.broadcasted_iota(jnp.int32, (1, width), 1)
        return (ids < limit).astype(F32).astype(BF16)

    def side(level, other):
        return Picked(
            right,
            (None, half_r, width),
            lambda i, *meta: (spot(meta, level), core_of(meta) ^ other, 0),
        )

    def side_value(meta, ref, level):
        return ref[...] * keep(jnp.where(owns(meta, level), width, 0))

    def tile(of, level, other=None):
        if other is None:
            return Picked(
                panels, (None, None, width, width), lambda i, *meta: (of, spot(meta, level), 0, 0)
            )
        return Picked(
            panels,
            (None, None, half_w, width),
            lambda i, *meta: (of, spot(meta, level), core_of(meta) ^ other, 0),
        )

    def tile_value(meta, ref, of, level):
        return ref[...] * keep(live_owned(meta, of, level))

    def run(body, operands, outs, scratch=(), steps=1, after=(), limit=40):
        arrays, specs, moved = [], [], 0
        for operand in operands:
            if isinstance(operand, InHbm):
                arrays.append(operand.array)
                specs.append(pl.BlockSpec(memory_space=pltpu.HBM))
                continue
            if not isinstance(operand, Picked):
                zeros = (0,) * operand.ndim
                operand = Picked(operand, operand.shape, lambda i, sup, live_counts, zeros=zeros: zeros)
            arrays.append(operand.array)
            specs.append(pl.BlockSpec(operand.block, operand.index))
            size = operand.array.dtype.itemsize
            for n in operand.block:
                size *= n or 1
            moved += size * steps
        taken = len(arrays)
        arrays += list(after)
        specs += [pl.BlockSpec(memory_space=pl.ANY)] * len(after)

        def kernel(sup, live_counts, *refs):
            body((sup, live_counts), *refs[:taken], *refs[taken + len(after) :])

        single = not isinstance(outs, (list, tuple))
        listed = [outs] if single else list(outs)
        out_specs = [
            pl.BlockSpec(out.shape, lambda i, sup, live_counts, zeros=(0,) * len(out.shape): zeros)
            for out in listed
        ]
        moved += sum(out.size * out.dtype.itemsize for out in listed)
        results = pl.pallas_call(
            kernel,
            grid_spec=pltpu.PrefetchScalarGridSpec(
                num_scalar_prefetch=2,
                grid=(steps,),
                in_specs=specs,
                out_specs=out_specs,
                scratch_shapes=list(scratch),
            ),
            out_shape=listed,
            name=body.__name__,
            compiler_params=pltpu.CompilerParams(vmem_limit_bytes=limit * 1024 * 1024),
            cost_estimate=pl.CostEstimate(flops=0, bytes_accessed=moved, transcendentals=0),
        )(sup_rows, counts, *arrays)
        return results[0] if single else list(results)

    def spread(block):
        for bits in outer:
            block = block + swap(block, "row", bits)
        return block

    steps_up = [CORES * m for m in range(1, chips)]
    rows_half = shaped((half_r, width))
    lanes = part_w
    blocks = width // lanes

    def at(index, size):
        return pl.ds(pl.multiple_of(index * size, size), size)

    first_rows = 2 * half_r + 2 * half_w

    def first_send(meta, sides, tiles, send, kept, sem):
        core = core_of(meta)
        copies, start = [], 0
        for source, level in ((None, 0), (None, 1), (0, 1), (2, 3)):
            size = half_r if source is None else half_w
            whole = sides if source is None else tiles.at[source]
            for out, side_of in ((send, 1 - core), (kept, core)):
                copies.append(
                    pltpu.make_async_copy(
                        whole.at[spot(meta, level), at(side_of, size)],
                        out.at[start : start + size],
                        sem.at[len(copies)],
                    )
                )
            start += size
        for copy in copies:
            copy.start()
        for copy in copies:
            copy.wait()
        for out in (send, kept):
            for level in range(2):
                rows = slice(level * half_r, (level + 1) * half_r)
                out[rows] = out[rows] * keep(jnp.where(owns(meta, level), width, 0))
            for i, (of, level) in enumerate(((0, 1), (2, 3))):
                rows = slice(2 * half_r + i * half_w, 2 * half_r + (i + 1) * half_w)
                out[rows] = out[rows] * keep(live_owned(meta, of, level))

    first_shape = shaped((first_rows, width))
    first_out, first_kept = run(
        first_send,
        [InHbm(right), InHbm(panels)],
        [first_shape, first_shape],
        [pltpu.SemaphoreType.DMA((8,))],
        limit=52,
    )
    first_got = swap(first_out, "row", 1)

    b0_rows, column_rows = blocks * half_r, half_r + half_w
    near, far = (CORES, 2 * CORES)

    def first_split(meta, own, got, send, kept, p23_send, p23_kept, whole):
        whole[...] = own[...] + got[...]
        for i in range(blocks):
            send[i * half_r : (i + 1) * half_r] = whole[:half_r, i * lanes : (i + 1) * lanes]
        kept[:b0_rows] = send[:b0_rows]
        chip = chip_of(meta)
        for i, (mine, other) in enumerate(((0, 1), (2, 3))):
            rows = slice(b0_rows + i * column_rows, b0_rows + (i + 1) * column_rows)
            source = slice(half_r, half_r + column_rows)
            send[rows] = whole[source, at(chip ^ other, lanes)]
            kept[rows] = whole[source, at(chip ^ mine, lanes)]
            rows = slice(i * half_w, (i + 1) * half_w)
            source = slice(half_r + column_rows, first_rows)
            p23_send[rows] = whole[source, at(chip ^ other, lanes)]
            p23_kept[rows] = whole[source, at(chip ^ mine, lanes)]

    near_shape, p23_pair = (
        shaped((b0_rows + 2 * column_rows, lanes)),
        shaped((2 * half_w, lanes)),
    )
    near_send, near_kept, p23_send, p23_kept = run(
        first_split,
        [first_kept, first_got],
        [near_shape, near_shape, p23_pair, p23_pair],
        [pltpu.VMEM((first_rows, width), BF16)],
    )
    near_got = swap(spread(near_send), "row", near)
    near_kept = spread(near_kept)
    p23_got = swap(spread(p23_send), "row", near)
    p23_kept = spread(p23_kept)

    def panel_of(level, m):
        return Picked(
            panels,
            (None, None, width, width),
            lambda i, *meta: (level, leaf_of(meta) ^ m, 0, 0),
        )

    def panel_value(meta, ref, level, m):
        return ref[...] * keep(live(meta, level, leaf_of(meta) ^ m))

    orders = ((2, 1, 2), (3, 2, 1))
    panel_got, first_sent = [], []
    for level, one, two in orders:
        def panel_send(meta, pa, pb, out, level=level, one=one, two=two):
            out[0] = panel_value(meta, pa, level, one)
            out[1] = panel_value(meta, pb, level, one ^ two)

        sent = run(
            panel_send,
            [panel_of(level, one), panel_of(level, one ^ two)],
            shaped((2, width, width)),
            after=[near_send],
        )
        first_sent.append(sent)
        panel_got.append(swap(sent, "leaf", one))

    def first_join(meta, kept, got, send, own):
        send[:b0_rows] = kept[:b0_rows] + got[:b0_rows]
        middle = b0_rows + column_rows
        own[...] = kept[b0_rows:middle] + got[b0_rows:middle]
        send[b0_rows:] = kept[middle:] + got[middle:]

    far_send, columns_own = run(
        first_join,
        [near_kept, near_got],
        [shaped((b0_rows + column_rows, lanes)), shaped((column_rows, lanes))],
        after=[*first_sent],
    )
    far_got = swap(far_send, "row", far)

    def p23_join(meta, kept, got, send, own):
        own[...] = kept[:half_w] + got[:half_w]
        send[...] = kept[half_w:] + got[half_w:]

    p23_block = shaped((half_w, lanes))
    p23_send, p23_own = run(
        p23_join, [p23_kept, p23_got], [p23_block, p23_block], after=[far_send]
    )
    p23_far = swap(p23_send, "row", far)

    rest_got, linked_got = [], []
    for level in (2, 3):
        def rest_send(meta, b, p0, p1, out, linked_out, level=level):
            out[:half_r] = side_value(meta, b, level)
            out[half_r:] = tile_value(meta, p0, 0, level)
            linked_out[...] = tile_value(meta, p1, 1, level)

        rest_sent, linked_sent = run(
            rest_send,
            [side(level, 1), tile(0, level), tile(1, level)],
            [shaped((half_r + width, width)), shaped((width, width))],
            after=[near_send],
        )
        rest_got.append(swap(rest_sent, "row", 1))
        linked_got.append(swap(linked_sent, "row", 1))

    def solve0(meta, sent, got, own, diag, x0, p, b):
        x = jnp.zeros((half_r, width), F32)
        for i in range(blocks):
            rows = slice(i * half_r, (i + 1) * half_r)
            x = x + dot(sent[rows] + got[rows], diag[0, i * lanes : (i + 1) * lanes])
        x0[...] = x.astype(BF16)
        b[...] = own[:half_r] + got[b0_rows : b0_rows + half_r]
        p[...] = own[half_r:] + got[b0_rows + half_r :]

    x0, p01, b1 = run(
        solve0,
        [far_send, far_got, columns_own, diag_leaf],
        [rows_half, shaped((half_w, lanes)), shaped((half_r, lanes))],
        after=[p23_send],
    )
    x0_other = swap(x0, "row", 1)
    p01_other = swap(p01, "row", 1)

    def term1(meta, x0, p, p_other, b, t1, whole):
        core = core_of(meta)
        whole[at(core, half_w)] = p[...]
        whole[at(1 - core, half_w)] = p_other[...]
        t1[...] = b[...].astype(F32) - dot(x0[...], whole[...])

    t1 = run(
        term1,
        [x0, p01, p01_other, b1],
        shaped((half_r, lanes), F32),
        [pltpu.VMEM((width, lanes), BF16)],
        after=[p23_far],
    )
    panel_far, panel_sent = [], []
    for (level, one, two), got in zip(orders, panel_got):
        def panel_join(meta, p, got, out, level=level, two=two):
            value = panel_value(meta, p, level, two).astype(F32) + got[1].astype(F32)
            out[...] = value.astype(BF16)

        sent = run(
            panel_join, [panel_of(level, two), got], shaped((width, width)), after=[t1]
        )
        panel_sent.append(sent)
        panel_far.append(swap(sent, "leaf", two))

    p23 = p23_own + p23_far
    p23 = (p23.astype(F32) + swap(p23, "leaf", 1).astype(F32)).astype(BF16)
    p23_turned = swap(p23, "leaf", 2)

    def m1_sum(meta, a, b, out):
        out[...] = (a[...] + b[...]).astype(BF16)

    m1 = run(m1_sum, [t1, swap(t1, "leaf", 1)], shaped((half_r, lanes)), after=[])
    m1 = jnp.concatenate([m1, swap(m1, "row", near)])
    m1_far = swap(m1, "row", far)
    p23 = (p23.astype(F32) + p23_turned.astype(F32)).astype(BF16)
    p23_next = swap(p23, "row", near)

    def early(meta, *refs):
        x0, us = refs[6], refs[7:]
        for i in range(2):
            b, p0, got = refs[3 * i : 3 * i + 3]
            value = (side_value(meta, b, 2 + i) + got[:half_r]).astype(F32)
            us[i][...] = value - dot(x0[...], tile_value(meta, p0, 0, 2 + i) + got[half_r:])

    us = run(
        early,
        [side(2, 0), tile(0, 2), rest_got[0], side(3, 0), tile(0, 3), rest_got[1], x0],
        [shaped((half_r, width), F32)] * 2,
        after=[t1],
    )

    def x1_t23(meta, *refs):
        (near_two, far_two, diag), us, ps, got = refs[:3], refs[3:5], refs[5:7], refs[7:9]
        x1, outs, whole = refs[9], refs[10:-1], refs[-1]
        chip = chip_of(meta)
        x = jnp.zeros((half_r, width), F32)
        for m in range(chips):
            part = (near_two, far_two)[m // 2][(m % 2) * half_r : (m % 2 + 1) * half_r]
            x = x + dot(part, diag[at(chip ^ m, lanes)])
        x = x.astype(BF16)
        x1[...] = x
        for i in range(2):
            cols = slice(i * width, (i + 1) * width)
            whole[:, cols] = us[i][...] - dot(x, tile_value(meta, ps[i], 1, 2 + i) + got[i][...])
        for m, out in enumerate(outs):
            out[...] = whole[at(chip ^ m, part_r)].astype(BF16)

    pair = Picked(diag_pair, (None, width, width), lambda i, *meta: (lax.div(leaf_of(meta), 2), 0, 0))
    strip = shaped((part_r, 2 * width))
    x1, *strips = run(
        x1_t23,
        [m1, m1_far, pair] + us + [tile(1, 2), tile(1, 3)] + linked_got,
        [rows_half] + [strip] * chips,
        [pltpu.VMEM((half_r, 2 * width), F32)],
        after=[*panel_sent],
    )
    strips[1:] = [swap(piece, "row", step) for piece, step in zip(strips[1:], steps_up)]
    x01_other = [x0_other, swap(x1, "row", 1)]

    ways = ((1, 2), (2, 1))

    def leaf_tile(array, level):
        if level is None:
            return Picked(array, (None, height, width), lambda i, *meta: (leaf_of(meta) ^ i, 0, 0))
        return Picked(
            array, (None, None, width, width), lambda i, *meta: (level, leaf_of(meta) ^ i, 0, 0)
        )

    def update01(meta, b, pa, pb, x0, x1, x0_other, x1_other, *refs):
        sends, kept, whole = refs[:2], refs[2:4], refs[4]
        step = pl.program_id(0)
        core = core_of(meta)
        a = leaf_of(meta) ^ step

        @pl.when(step == 0)
        def _():
            for i, (mine, other) in enumerate(((x0, x0_other), (x1, x1_other))):
                whole[i, at(core, half_r)] = mine[...]
                whole[i, at(1 - core, half_r)] = other[...]

        value = b[...].astype(F32)
        for i, p in enumerate((pa, pb)):
            value = value - dot(whole[i], p[...] * keep(live(meta, i, a)))
        for half, (one, two) in enumerate(ways):
            part = value[half * half_r : (half + 1) * half_r]
            for i, m in enumerate((one, one ^ two)):
                @pl.when(step == m)
                def _(half=half, i=i, part=part):
                    sends[half][i] = part.astype(BF16)
            for i, m in enumerate((0, two)):
                @pl.when(step == m)
                def _(half=half, i=i, part=part):
                    kept[half][i] = part

    share_pair = (2, half_r, width)
    share_send0, share_send1, share_kept0, share_kept1 = run(
        update01,
        [leaf_tile(right, None), leaf_tile(panels, 0), leaf_tile(panels, 1), x0, x1] + x01_other,
        [shaped(share_pair)] * 2 + [shaped(share_pair, F32)] * 2,
        [pltpu.VMEM((2, height, width), BF16)],
        steps=n_leaf,
    )
    share_got = [swap(share_send0, "leaf", ways[0][0]), swap(share_send1, "leaf", ways[1][0])]

    def share_join(meta, kept0, kept1, got0, got1, out0, out1):
        for kept, got, out in ((kept0, got0, out0), (kept1, got1, out1)):
            out[...] = (kept[1] + got[1].astype(F32)).astype(BF16)

    share_sent = run(
        share_join, [share_kept0, share_kept1] + share_got, [shaped((half_r, width))] * 2
    )
    share_far = [swap(sent, "leaf", way[1]) for sent, way in zip(share_sent, ways)]

    def t23_sum(meta, *refs):
        value = refs[0][...]
        for ref in refs[1:-1]:
            value = value + ref[...]
        refs[-1][...] = value

    t23 = spread(run(t23_sum, strips, strip, after=[share_send0]))
    def p23_stack(meta, a, b, out):
        out[:half_w] = a[...]
        out[half_w:] = b[...]

    p23 = run(p23_stack, [p23, p23_next], p23_pair, after=[x1])
    p23_far = swap(p23, "row", far)

    def p23_place(meta, near_two, far_two, out):
        for m in range(chips):
            source = (near_two, far_two)[m // 2]
            rows = slice((m % 2) * half_w, (m % 2 + 1) * half_w)
            out[:, at(chip_of(meta) ^ m, lanes)] = source[rows]

    p23_half = run(p23_place, [p23, p23_far], shaped((half_w, width)))
    p23_other = swap(p23_half, "row", 1)

    t23 = t23.astype(F32) + swap(t23, "leaf", 1).astype(F32)
    t23_far = swap(t23, "leaf", 2)

    def m23_sum(meta, a, b, out):
        out[...] = (a[...] + b[...]).astype(BF16)

    m23 = run(
        m23_sum,
        [t23, t23_far],
        strip,
        after=[p23_half, *share_sent],
    )
    m23_parts = [m23] + [swap(m23, "row", step) for step in steps_up]

    def leaf_sums(meta, pa, pb, ga, gb, fa, fb, k0, k1, g0, g1, f0, f1, panel_out, share_out):
        for i, (p, got, far) in enumerate(((pa, ga, fa), (pb, gb, fb))):
            value = panel_value(meta, p, 2 + i, 0).astype(F32)
            panel_out[i] = (value + got[0].astype(F32) + far[...].astype(F32)).astype(BF16)
        for i, (kept, got, far) in enumerate(((k0, g0, f0), (k1, g1, f1))):
            value = kept[0] + got[0].astype(F32) + far[...].astype(F32)
            share_out[i * half_r : (i + 1) * half_r] = value

    panel_sum, share_sum = run(
        leaf_sums,
        [panel_of(2, 0), panel_of(3, 0)]
        + panel_got
        + panel_far
        + [share_kept0, share_kept1]
        + share_got
        + share_far,
        [shaped((2, width, width)), shaped((height, width), F32)],
    )

    def x2_x3(meta, *refs):
        parts, (diag, p, p_other, out, whole, tile23) = refs[:chips], refs[chips:]
        chip, core = chip_of(meta), core_of(meta)
        for m, part in enumerate(parts):
            whole[at(chip ^ m, part_r)] = part[...]
        tile23[at(core, half_w)] = p[...]
        tile23[at(1 - core, half_w)] = p_other[...]
        x = dot(whole[:, :width], diag[0]).astype(BF16)
        out[0] = x
        merged = whole[:, width:].astype(F32) - dot(x, tile23[...])
        out[1] = dot(merged.astype(BF16), diag[1]).astype(BF16)

    x23 = run(
        x2_x3,
        m23_parts + [diag_root, p23_half, p23_other],
        shaped((2, half_r, width)),
        [pltpu.VMEM((half_r, 2 * width), BF16), pltpu.VMEM((width, width), BF16)],
        after=[panel_sum],
    )
    x23_other = swap(x23, "row", 1)

    def final(meta, x23, x23_other, panel, share, top, bottom, whole):
        core = core_of(meta)
        value = share[...]
        for i in range(2):
            whole[i, at(core, half_r)] = x23[i]
            whole[i, at(1 - core, half_r)] = x23_other[i]
            value = value - dot(whole[i], panel[i])
        top[...] = value[:half_r].astype(BF16)
        bottom[...] = value[half_r:].astype(BF16)

    top, bottom = run(
        final,
        [x23, x23_other, panel_sum, share_sum],
        [rows_half, rows_half],
        [pltpu.VMEM((2, height, width), BF16)],
    )

    def write_solved(meta, x0, x1, x0_other, x1_other, x23, x23_other, out):
        core = core_of(meta)
        mine, other = at(core, half_r), at(1 - core, half_r)
        for i, (a, b) in enumerate(((x0, x0_other), (x1, x1_other))):
            out[i, mine] = a[...]
            out[i, other] = b[...]
        for i in range(2):
            out[2 + i, mine] = x23[i]
            out[2 + i, other] = x23_other[i]

    solved = run(
        write_solved,
        [x0, x1] + x01_other + [x23, x23_other],
        shaped((levels, height, width)),
        after=[top],
    )

    top_1, bottom_2 = swap(top, "leaf", 1), swap(bottom, "leaf", 2)
    bottom_1, top_2 = swap(bottom, "leaf", 1), swap(top, "leaf", 2)
    top_3, bottom_3 = swap(top_1, "leaf", 2), swap(bottom_2, "leaf", 1)

    def write_updated(meta, *refs):
        parts, out = refs[:-1], refs[-1]
        for m in range(n_leaf):
            for half in range(2):
                rows = slice(half * half_r, (half + 1) * half_r)
                out[leaf_of(meta) ^ m, rows] = parts[2 * m + half][...]

    updated = run(
        write_updated,
        [top, bottom, top_1, bottom_1, top_2, bottom_2, top_3, bottom_3],
        shaped((n_leaf, height, width)),
        after=[],
    )
    return solved[:, None], updated


def solution(mesh):
    return jax.shard_map(
        on_device,
        mesh=mesh,
        in_specs=(
            P("leaf", "row", None, None),
            P(None, "leaf", "row", None, None),
            P(None, "leaf", "row"),
            P("leaf", None, None),
            P(),
            P(),
            P(),
        ),
        out_specs=(P(None, "leaf", None, None), P("row", None, None)),
        check_vma=False,
    )
```
